256 devices in a mesh: tm: 8 (over x, core), seq: 32 (over y, z).
Axes of the slice: x: 4, y: 4, z: 8, core: 2. Of those that a mesh axis runs over, the one named last changes fastest.
Arguments:
- rgb_feat: bfloat16 [8, 16384, 1024], P('tm', 'seq'), may hold values from -60 to 60
- rgb_grad_out: bfloat16 [8, 16384, 1024], P('tm', 'seq'), may hold values from -6 to 6
- pose_feat: bfloat16 [8, 4096, 1024], P('tm', 'seq'), may hold values from -12 to 12
- pose_grad_out: bfloat16 [8, 4096, 1024], P('tm', 'seq'), may hold values from -6 to 6
- logit_scale: float32 [8], replicated, may hold values from 0.5 to 2.5
- pairs: int32 [8, 160], P('tm', 'seq'), may hold values from -1 to 127, as said below
Outputs:
- rgb_grad: bfloat16 [8, 16384, 1024], P('tm', 'seq')
- pose_grad: bfloat16 [8, 4096, 1024], P('tm', 'seq')
- scale_grad: float32 [8], replicated
The draws below stay inside these ranges and needn't reach their ends.
Inputs may be any that keep to these rules, and one draw needn't show every extreme that they name: `pairs`: each entry is -1 or rgb_tile * 32 + pose_tile with rgb_tile below 4, naming one of the device's own RGB tiles and the pose tile of seq index pose_tile of the same time group. Live entries come first and never repeat within a device's list; in every time group some device has all 5 entries live.
All inputs are finite; a program needn't handle non-finite values.
Results may differ from the reference program's by a relative error of at most 0.023.
Values may be sent and summed in bfloat16 or wider, within the bound.
A program may use at most 128 MiB of HBM per device.

```python
import math
import jax
import jax.numpy as jnp
from jax import lax

HEADS = 8
HEAD_DIM = 128
TILE = 128
RGB_DEV = 512
PAIRS_DEV = 5
WIDTH = 1024
RGB_TILES = 4
RGB_ROWS = 16384
POSE_ROWS = 4096
N_TM = 8
N_SEQ = 32


def row_scales(seed_key, rows, highest):
    return jnp.exp(jax.random.uniform(seed_key, (N_TM, rows, 1), jnp.float32) * jnp.log(highest))


def pose_source(seed_key, highest):
    normal_part = jax.random.normal(jax.random.fold_in(seed_key, 101), (N_TM, POSE_ROWS, WIDTH), jnp.float32)
    clipped = jnp.clip(normal_part, -4.0, 4.0)
    return clipped * row_scales(jax.random.fold_in(seed_key, 102), POSE_ROWS, highest)


def draw_pose_feat(key, part):
    values = pose_source(key, 1.0)
    return values.astype(jnp.bfloat16)


def draw_rgb_feat(key, part):
    key = jax.random.fold_in(key, 9)
    values = jnp.clip(jax.random.normal(key, (N_TM, RGB_ROWS, WIDTH), jnp.float32), -4.0, 4.0)
    return values.astype(jnp.bfloat16)


def draw_pairs(key, part):
    key = jax.random.fold_in(key, 3)
    combos = RGB_TILES * N_SEQ
    first_key, second_key, third_key = jax.random.split(key, 3)
    ranking = jax.random.randint(first_key, (N_TM, N_SEQ, combos), 0, 65536) * combos + jnp.arange(combos)[None, None, :]
    picked = jnp.argsort(ranking, axis=-1)[:, :, :PAIRS_DEV]
    counts = jax.random.randint(second_key, (N_TM, N_SEQ), 2, PAIRS_DEV // 2 + 2)
    busiest = jax.random.randint(third_key, (N_TM,), 0, N_SEQ)
    counts = jnp.where(jnp.arange(N_SEQ)[None, :] == busiest[:, None], PAIRS_DEV, counts)
    is_live = jnp.arange(PAIRS_DEV)[None, None, :] < counts[:, :, None]
    pair_codes = jnp.where(is_live, picked, -1)
    return pair_codes.reshape(N_TM, N_SEQ * PAIRS_DEV).astype(jnp.int32)


def block_scale(key, shape, cuts, low, top_value):
    factor_of = 1.0
    for dim, parts in cuts:
        draws = jax.random.uniform(jax.random.fold_in(jax.random.fold_in(key, 6), dim), (parts,), jnp.float32, low / len(cuts), top_value / len(cuts))
        factor_of = factor_of * jnp.repeat(jnp.exp(draws), shape[dim] // parts).reshape((-1,) + (1,) * (len(shape) - 1 - dim))
    return factor_of


def normal_values(rng, shape, width, bound, pieces=(), kind=jnp.bfloat16):
    level = block_scale(rng, shape, pieces, -0.22, 0.18) if pieces else 1.0
    array = jax.random.normal(rng, shape, jnp.float32) * width * level
    return jnp.minimum(jnp.maximum(array, -bound), bound).astype(kind)


def setup_inputs(seed: int = 0) -> dict:
    splits = jax.random.split(jax.random.key(seed), 7)
    rgb_feat = draw_rgb_feat(jax.random.fold_in(splits[6], 71), 0)
    rgb_grad_out = normal_values(splits[1], (N_TM, RGB_ROWS, WIDTH), 1.0, 6.0, ((0, 8), (1, 32)))
    pose_feat = draw_pose_feat(jax.random.fold_in(splits[6], 71), 0)
    pose_grad_out = normal_values(splits[3], (N_TM, POSE_ROWS, WIDTH), 1.0, 6.0, ((0, 8), (1, 32)))
    logit_scale = jnp.clip(jnp.exp(jax.random.uniform(splits[4], (HEADS,), jnp.float32, math.log(0.5), math.log(2.5))), 0.5, 2.5)
    pairs = draw_pairs(jax.random.fold_in(splits[6], 71), 0)
    return dict(rgb_feat=rgb_feat, rgb_grad_out=rgb_grad_out, pose_feat=pose_feat, pose_grad_out=pose_grad_out, logit_scale=logit_scale, pairs=pairs)


NEG = -1e+30

def split_heads(values):
    return values.reshape(values.shape[:-1] + (HEADS, HEAD_DIM))

def product(pattern, former, latter):
    return jnp.einsum(pattern, former.astype(jnp.float32), latter.astype(jnp.float32), precision=lax.Precision.HIGHEST)

def group_max(hot_table, values):
    return lax.optimization_barrier(jnp.max(jnp.where(hot_table[:, :, None, None], values[:, None], NEG), axis=0))

def group_sum(hot_table, values):
    return jnp.einsum('pt,p...->t...', hot_table.astype(values.dtype), values, precision=lax.Precision.HIGHEST)

def pick_tiles(rgb_rows, rgb_cot, pose_rows, pose_cot, pair_codes):
    is_live = pair_codes >= 0
    clamped = jnp.maximum(pair_codes, 0).astype(jnp.int32)
    rgb_index = (clamped // N_SEQ).astype(jnp.int32)
    pose_index = (clamped % N_SEQ).astype(jnp.int32)
    rgb_blocks = rgb_rows.reshape(RGB_TILES, TILE, WIDTH)[rgb_index]
    rgb_cots = rgb_cot.reshape(RGB_TILES, TILE, WIDTH)[rgb_index]
    pose_blocks = pose_rows.reshape(N_SEQ, TILE, WIDTH)[pose_index]
    pose_cots = pose_cot.reshape(N_SEQ, TILE, WIDTH)[pose_index]
    rgb_hot = (rgb_index[:, None] == jnp.arange(RGB_TILES).astype(jnp.int32)[None, :]) & is_live[:, None]
    pose_hot = (pose_index[:, None] == jnp.arange(N_SEQ).astype(jnp.int32)[None, :]) & is_live[:, None]
    return (is_live, rgb_index, pose_index, rgb_blocks, rgb_cots, pose_blocks, pose_cots, rgb_hot, pose_hot)

def score_tiles(rgb_blocks, pose_blocks, pose_cots, logit_scale):
    split_rgb = split_heads(rgb_blocks)
    raw_dot = product('pihe,pjhe->phij', split_rgb, split_heads(pose_blocks)) / math.sqrt(HEAD_DIM)
    scores = raw_dot * logit_scale[None, :, None, None]
    pose_dot = product('pihe,pjhe->phij', split_rgb, split_heads(pose_cots))
    return (raw_dot, scores, pose_dot)

def pose_partials(scores, pose_dot, is_live, pose_index, pose_hot):
    live_four = is_live[:, None, None, None]
    col_max = jnp.where(is_live[:, None, None], lax.optimization_barrier(jnp.max(scores, axis=2)), NEG)
    part_max = group_max(pose_hot, col_max)
    col_weights = jnp.where(live_four, jnp.exp(scores - part_max[pose_index][:, :, None, :]), 0.0)
    part_sum = group_sum(pose_hot, lax.optimization_barrier(jnp.sum(col_weights, axis=2)))
    part_dot = group_sum(pose_hot, lax.optimization_barrier(jnp.sum(col_weights * pose_dot, axis=2)))
    return (part_max, part_sum, part_dot)

def device_terms(tile_set, logit_scale, pose_max, pose_den, pose_gam):
    is_live, rgb_index, pose_index, rgb_blocks, rgb_cots, pose_blocks, pose_cots, rgb_hot, pose_hot = tile_set
    raw_dot, scores, pose_dot = score_tiles(rgb_blocks, pose_blocks, pose_cots, logit_scale)
    live_four = is_live[:, None, None, None]
    row_max = jnp.where(is_live[:, None, None], lax.optimization_barrier(jnp.max(scores, axis=3)), NEG)
    pair_max = group_max(rgb_hot, row_max)[rgb_index]
    row_weights = jnp.where(live_four, jnp.exp(scores - pair_max[..., None]), 0.0)
    rgb_den = jnp.maximum(group_sum(rgb_hot, lax.optimization_barrier(jnp.sum(row_weights, axis=3))), 1.0)[rgb_index]
    rgb_prob = jnp.where(live_four, jnp.exp(scores - pair_max[..., None]) / rgb_den[..., None], 0.0)
    pose_prob = jnp.where(live_four, jnp.exp(scores - pose_max[pose_index][:, :, None, :]) / pose_den[pose_index][:, :, None, :], 0.0)
    grad_p = product('pihe,pjhe->phij', split_heads(rgb_cots), split_heads(pose_blocks))
    row_delta = group_sum(rgb_hot, lax.optimization_barrier(jnp.sum(rgb_prob * grad_p, axis=3)))[rgb_index]
    dscore = rgb_prob * (grad_p - row_delta[..., None]) + pose_prob * (pose_dot - pose_gam[pose_index][:, :, None, :])
    dscore_low = dscore.astype(jnp.bfloat16)
    rgb_low = rgb_prob.astype(jnp.bfloat16)
    pose_low = pose_prob.astype(jnp.bfloat16)
    head_scale = (logit_scale / math.sqrt(HEAD_DIM))[None, None, :, None]
    rgb_part = product('phij,pjhe->pihe', pose_low, split_heads(pose_cots)) + head_scale * product('phij,pjhe->pihe', dscore_low, split_heads(pose_blocks))
    pose_part = product('phij,pihe->pjhe', rgb_low, split_heads(rgb_cots)) + head_scale * product('phij,pihe->pjhe', dscore_low, split_heads(rgb_blocks))
    rgb_rows = group_sum(rgb_hot, rgb_part).reshape(RGB_TILES * TILE, WIDTH)
    pose_terms = group_sum(pose_hot, pose_part).reshape(N_SEQ * TILE, WIDTH)
    scale_term = lax.optimization_barrier(jnp.sum(dscore * raw_dot, axis=(0, 2, 3)))
    return (rgb_rows, pose_terms, scale_term)

def group_terms(rgb_rows, rgb_cot, pose_rows, pose_cot, pair_codes, logit_scale):
    rgb_dev = rgb_rows.reshape(N_SEQ, RGB_DEV, WIDTH)
    cot_dev = rgb_cot.reshape(N_SEQ, RGB_DEV, WIDTH)
    codes_dev = pair_codes.reshape(N_SEQ, PAIRS_DEV)

    def stats_of(inputs):
        tile_set = pick_tiles(inputs[0], inputs[1], pose_rows, pose_cot, inputs[2])
        raw_dot, scores, pose_dot = score_tiles(tile_set[3], tile_set[5], tile_set[6], logit_scale)
        return pose_partials(scores, pose_dot, tile_set[0], tile_set[2], tile_set[8])
    part_max, part_sum, part_dot = lax.map(stats_of, (rgb_dev, cot_dev, codes_dev))
    pose_max = lax.optimization_barrier(jnp.max(part_max, axis=0))
    factor = jnp.exp(part_max - pose_max[None])
    pose_den = jnp.maximum(lax.optimization_barrier(jnp.sum(part_sum * factor, axis=0)), 1.0)
    pose_gam = lax.optimization_barrier(jnp.sum(part_dot * factor, axis=0)) / pose_den

    def device_step(running, inputs):
        pose_acc, scale_acc = running
        tile_set = pick_tiles(inputs[0], inputs[1], pose_rows, pose_cot, inputs[2])
        rgb_out, pose_terms, scale_term = device_terms(tile_set, logit_scale, pose_max, pose_den, pose_gam)
        rounded = lax.optimization_barrier(pose_terms.astype(jnp.bfloat16))
        return ((pose_acc + rounded.astype(jnp.float32), scale_acc + scale_term), rgb_out.astype(jnp.bfloat16))
    start_state = (jnp.zeros((POSE_ROWS, WIDTH), jnp.float32), jnp.zeros((HEADS,), jnp.float32))
    finals, rgb_out = lax.scan(device_step, start_state, (rgb_dev, cot_dev, codes_dev))
    return (rgb_out.reshape(RGB_ROWS, WIDTH), finals[0].astype(jnp.bfloat16), finals[1])

def reference(rgb_feat, rgb_grad_out, pose_feat, pose_grad_out, logit_scale, pairs):

    def one_group(inputs):
        return group_terms(inputs[0], inputs[1], inputs[2], inputs[3], inputs[4], logit_scale)
    rgb_grad, pose_grad, scale_parts = lax.map(one_group, (rgb_feat, rgb_grad_out, pose_feat, pose_grad_out, pairs))
    return (rgb_grad, pose_grad, lax.optimization_barrier(jnp.sum(scale_parts, axis=0)))
```

```python
import functools
import math

import jax
import jax.numpy as jnp
from jax import lax
from jax.experimental import pallas as pl
from jax.experimental.pallas import tpu as pltpu
from jax.sharding import PartitionSpec as P

NEG = -1e30
NY = 4
NZ = 8
NT = 8
TILE = 128
HD = 128
SLOTS = 5
WIDE = 256
VMEM_LIMIT = 56 * 1024 * 1024
MESH = pl.DeviceIdType.MESH
ANY = pl.BlockSpec(memory_space=pl.ANY)
VM = pl.BlockSpec(memory_space=pltpu.VMEM)
SM = pl.BlockSpec(memory_space=pltpu.SMEM)


def place():
    me = lax.axis_index("seq")
    return me // NZ, me % NZ


def remote(src, dst, send_sem, recv_sem, y, z):
    return pltpu.make_async_remote_copy(
        src_ref=src,
        dst_ref=dst,
        send_sem=send_sem,
        recv_sem=recv_sem,
        device_id={"seq": y * NZ + z},
        device_id_type=MESH,
    )


def remote_tm(src, dst, send_sem, recv_sem, t):
    return pltpu.make_async_remote_copy(
        src_ref=src,
        dst_ref=dst,
        send_sem=send_sem,
        recv_sem=recv_sem,
        device_id={"tm": t},
        device_id_type=MESH,
    )


def greet(seqs, tms=()):
    barrier = pltpu.get_barrier_semaphore()
    for y, z in seqs:
        pl.semaphore_signal(
            barrier, inc=1, device_id={"seq": y * NZ + z}, device_id_type=MESH
        )
    for t in tms:
        pl.semaphore_signal(barrier, inc=1, device_id={"tm": t}, device_id_type=MESH)
    pl.semaphore_wait(barrier, len(seqs) + len(tms))


def columns(y):
    return pl.ds(pl.multiple_of(y * WIDE, WIDE), WIDE)


def gather_kernel(
    rgb_ref, cot_ref, pf_ref, pc_ref, pairs_ref,
    rgbx, cotx, pose, pairs_x,
    local_sem, y_send, y_recv, z_send, z_recv,
):
    y, z = place()
    greet(
        [((y + k) % NY, z) for k in (1, 2, 3)]
        + [(y, (z + 1) % NZ), (y, (z + NZ - 1) % NZ)]
    )

    def y_copies(k):
        to = (y + k) % NY
        cols = columns(to)
        parts = (
            (pf_ref.at[:, cols], pose.at[z * NY + y, 0]),
            (pc_ref.at[:, cols], pose.at[z * NY + y, 1]),
            (pairs_ref, pairs_x.at[y]),
            (rgb_ref.at[:, :, cols], rgbx.at[pl.ds(y * 4, 4)]),
            (cot_ref.at[:, :, cols], cotx.at[pl.ds(y * 4, 4)]),
        )
        if k == 0:
            return [
                pltpu.make_async_copy(src, dst, local_sem.at[i])
                for i, (src, dst) in enumerate(parts)
            ]
        return [
            remote(src, dst, y_send.at[k - 1, i], y_recv.at[k - 1, i], to, z)
            for i, (src, dst) in enumerate(parts)
        ]

    own = y_copies(0)
    across = {k: y_copies(k) for k in (1, 2, 3)}
    own[0].start()
    own[1].start()
    for i in range(3):
        for k in (1, 2, 3):
            across[k][i].start()
    own[2].start()

    def hop(side, step, c):
        block = (z + NZ - step) % NZ if side == 0 else (z + step) % NZ
        to = (z + 1) % NZ if side == 0 else (z + NZ - 1) % NZ
        ref = pose.at[block * NY + (y + NY - c) % NY]
        return remote(ref, ref, z_send.at[side, step, c], z_recv.at[side, step, c], y, to)

    def used(side, step, c):
        return step < 3 or (c < 2) == (side == 0)

    sent = []
    for step in range(4):
        for c in range(NY):
            if step == 0:
                if c == 0:
                    own[0].wait()
                    own[1].wait()
                else:
                    across[c][0].wait_recv()
                    across[c][1].wait_recv()
            for side in range(2):
                if step > 0:
                    hop(side, step - 1, c).wait_recv()
                if used(side, step, c):
                    copy = hop(side, step, c)
                    copy.start()
                    sent.append(copy)
            if step == 0 and c == 0:
                for i in (3, 4):
                    for k in (1, 2, 3):
                        across[k][i].start()
                    own[i].start()
    for c in range(NY):
        for side in range(2):
            if used(side, 3, c):
                hop(side, 3, c).wait_recv()
    for k in (1, 2, 3):
        for i in (2, 3, 4):
            across[k][i].wait_recv()
    for i in (2, 3, 4):
        own[i].wait()
    for k in (1, 2, 3):
        for i in range(5):
            across[k][i].wait_send()
    for copy in sent:
        copy.wait_send()


def gather(rgb, cot, pf, pc, pairs):
    return pl.pallas_call(
        gather_kernel,
        out_shape=(
            jax.ShapeDtypeStruct((16, TILE, WIDE), jnp.bfloat16),
            jax.ShapeDtypeStruct((16, TILE, WIDE), jnp.bfloat16),
            jax.ShapeDtypeStruct((NY * NZ, 2, TILE, WIDE), jnp.bfloat16),
            jax.ShapeDtypeStruct((NY, 1, SLOTS), jnp.int32),
        ),
        in_specs=[ANY] * 5,
        out_specs=(ANY,) * 4,
        scratch_shapes=[
            pltpu.SemaphoreType.DMA((5,)),
            pltpu.SemaphoreType.DMA((3, 5)),
            pltpu.SemaphoreType.DMA((3, 5)),
            pltpu.SemaphoreType.DMA((2, 4, 4)),
            pltpu.SemaphoreType.DMA((2, 4, 4)),
        ],
        compiler_params=pltpu.CompilerParams(
            collective_id=0, has_side_effects=True, vmem_limit_bytes=VMEM_LIMIT
        ),
    )(rgb, cot, pf, pc, pairs)


def dot_t(a, b):
    return lax.dot_general(a, b, (((1,), (1,)), ((), ())), preferred_element_type=jnp.float32)


def merge_into(ref, index, h, high, total, inner):
    old = ref[index, pl.ds(h, 1), :]
    top = jnp.maximum(old, high)
    keep = jnp.exp(old - top)
    add = jnp.exp(high - top)
    ref[index, pl.ds(h, 1), :] = top
    ref[index, pl.ds(2 + h, 1), :] = ref[index, pl.ds(2 + h, 1), :] * keep + total * add
    ref[index, pl.ds(4 + h, 1), :] = ref[index, pl.ds(4 + h, 1), :] * keep + inner * add


def pair_index(pairs, n):
    r = n // SLOTS
    code = pairs[r, 0, n % SLOTS]
    kept = jnp.maximum(code, 0)
    tile = kept % (NY * NZ)
    return code >= 0, r * 4 + kept // (NY * NZ), (tile % NZ) * NY + tile // NZ


def stats_kernel(pairs, scale, rgbx, cotx, pose, st, rs):
    row = lax.broadcasted_iota(jnp.int32, (1, 8, HD), 1)
    blank = jnp.where(row < 2, NEG, 0.0)
    st[...] = jnp.broadcast_to(blank, st.shape)
    rs[...] = jnp.broadcast_to(blank, rs.shape)

    def body(n, carry):
        live, ri, pi = pair_index(pairs, n)

        @pl.when(live)
        def _():
            for h in range(2):
                cols = pl.ds(h * HD, HD)
                factor = scale[h] / math.sqrt(HD)
                q = rgbx[ri, :, cols]
                g = cotx[ri, :, cols]
                both = pose[pi, :, :, cols].reshape(2 * TILE, HD)
                pf = pose[pi, 0, :, cols]
                dots = dot_t(q, both)
                score = dots[:, :TILE] * factor
                high = jnp.max(score, axis=0, keepdims=True)
                w = jnp.exp(score - high)
                merge_into(
                    st, pi, h, high,
                    jnp.sum(w, axis=0, keepdims=True),
                    jnp.sum(w * dots[:, TILE:], axis=0, keepdims=True),
                )
                score = dot_t(pf, q) * factor
                grad = dot_t(pf, g)
                high = jnp.max(score, axis=0, keepdims=True)
                w = jnp.exp(score - high)
                merge_into(
                    rs, ri, h, high,
                    jnp.sum(w, axis=0, keepdims=True),
                    jnp.sum(w * grad, axis=0, keepdims=True),
                )

        return carry

    lax.fori_loop(0, NY * SLOTS, body, 0)


def stats(pairs, scale, rgbx, cotx, pose):
    return pl.pallas_call(
        stats_kernel,
        out_shape=(
            jax.ShapeDtypeStruct((NY * NZ, 8, HD), jnp.float32),
            jax.ShapeDtypeStruct((16, 8, HD), jnp.float32),
        ),
        in_specs=[SM, SM, VM, VM, VM],
        out_specs=(VM, VM),
        compiler_params=pltpu.CompilerParams(vmem_limit_bytes=VMEM_LIMIT),
    )(pairs, scale, rgbx, cotx, pose)


def exchange_kernel(st, fin, got, send1, recv1, send2, recv2):
    y, z = place()
    greet([(y, (z + k) % NZ) for k in range(1, NZ)])

    def first(k):
        to = (z + k) % NZ
        return remote(
            st.at[pl.ds(to * NY, NY)], got.at[z], send1.at[k - 1], recv1.at[k - 1], y, to
        )

    def second(k):
        to = (z + k) % NZ
        ref = fin.at[pl.ds(z * NY, NY)]
        return remote(ref, ref, send2.at[k - 1], recv2.at[k - 1], y, to)

    for k in range(1, NZ):
        first(k).start()
    got[z] = st[pl.ds(z * NY, NY)]
    for k in range(1, NZ):
        first(k).wait_recv()
    top = got[0, :, 0:2, :]
    for k in range(1, NZ):
        top = jnp.maximum(top, got[k, :, 0:2, :])
    total = jnp.zeros_like(top)
    inner = jnp.zeros_like(top)
    for k in range(NZ):
        keep = jnp.exp(got[k, :, 0:2, :] - top)
        total += got[k, :, 2:4, :] * keep
        inner += got[k, :, 4:6, :] * keep
    inverse = 1.0 / jnp.maximum(total, 1.0)
    mine = pl.ds(z * NY, NY)
    fin[mine, 0:2, :] = top
    fin[mine, 2:4, :] = inverse
    fin[mine, 4:6, :] = inner * inverse
    fin[mine, 6:8, :] = jnp.zeros_like(top)
    for k in range(1, NZ):
        second(k).start()
    for k in range(1, NZ):
        second(k).wait_recv()
    for k in range(1, NZ):
        first(k).wait_send()
        second(k).wait_send()


def exchange(st):
    return pl.pallas_call(
        exchange_kernel,
        out_shape=jax.ShapeDtypeStruct((NY * NZ, 8, HD), jnp.float32),
        in_specs=[VM],
        out_specs=VM,
        scratch_shapes=[pltpu.VMEM((NZ, NY, 8, HD), jnp.float32)]
        + [pltpu.SemaphoreType.DMA((NZ - 1,))] * 4,
        compiler_params=pltpu.CompilerParams(
            collective_id=1, has_side_effects=True, vmem_limit_bytes=VMEM_LIMIT
        ),
    )(st)


def backward_kernel(
    pairs, scale, rgbx, cotx, pose, rs, fin, rgb_out, pose_out, scale_out, racc, pacc, sacc
):
    racc[...] = jnp.zeros_like(racc)
    pacc[...] = jnp.zeros_like(pacc)
    sacc[...] = jnp.zeros_like(sacc)

    def body(n, carry):
        live, ri, pi = pair_index(pairs, n)

        @pl.when(live)
        def _():
            rows = rs[ri]
            inverse = 1.0 / jnp.maximum(rows[2:4], 1.0)
            rows = jnp.concatenate(
                [rows[0:2], inverse, rows[4:6] * inverse, jnp.zeros((2, HD), jnp.float32)], axis=0
            )
            rows = jnp.transpose(rows)
            for h in range(2):
                cols = pl.ds(h * HD, HD)
                factor = scale[h] / math.sqrt(HD)
                q = rgbx[ri, :, cols]
                g = cotx[ri, :, cols]
                both = pose[pi, :, :, cols].reshape(2 * TILE, HD)
                pf = pose[pi, 0, :, cols]
                pc = pose[pi, 1, :, cols]
                dots = dot_t(q, both)
                raw = dots[:, :TILE]
                score = raw * factor
                grad = dot_t(g, pf)
                pr = jnp.exp(score - rows[:, h:h + 1]) * rows[:, 2 + h:3 + h]
                pp = jnp.exp(score - fin[pi, pl.ds(h, 1), :]) * fin[pi, pl.ds(2 + h, 1), :]
                ds = pr * (grad - rows[:, 4 + h:5 + h]) + pp * (
                    dots[:, TILE:] - fin[pi, pl.ds(4 + h, 1), :]
                )
                sacc[h] += jnp.sum((ds * raw).reshape(TILE // 8, 8, HD), axis=0)
                ds_low = ds.astype(jnp.bfloat16)
                pr_low = pr.astype(jnp.bfloat16)
                pp_low = pp.astype(jnp.bfloat16)
                racc[ri, :, cols] += jnp.dot(
                    pp_low, pc, preferred_element_type=jnp.float32
                ) + factor * jnp.dot(ds_low, pf, preferred_element_type=jnp.float32)
                turned = (((0,), (0,)), ((), ()))
                pacc[pi, :, cols] += lax.dot_general(
                    pr_low, g, turned, preferred_element_type=jnp.float32
                ) + factor * lax.dot_general(
                    ds_low, q, turned, preferred_element_type=jnp.float32
                )

        return carry

    lax.fori_loop(0, NY * SLOTS, body, 0)
    rgb_out[...] = racc[...].astype(jnp.bfloat16)
    pose_out[...] = pacc[...].astype(jnp.bfloat16)
    for h in range(2):
        part = jnp.sum(sacc[h], axis=0, keepdims=True)
        part = jnp.sum(part, axis=1, keepdims=True) / math.sqrt(HD)
        scale_out[pl.ds(h, 1), :] = jnp.broadcast_to(part, (1, HD))
    scale_out[pl.ds(2, 6), :] = jnp.zeros((6, HD), jnp.float32)


def backward(pairs, scale, rgbx, cotx, pose, rs, fin):
    return pl.pallas_call(
        backward_kernel,
        out_shape=(
            jax.ShapeDtypeStruct((16, TILE, WIDE), jnp.bfloat16),
            jax.ShapeDtypeStruct((NY * NZ, TILE, WIDE), jnp.bfloat16),
            jax.ShapeDtypeStruct((8, HD), jnp.float32),
        ),
        in_specs=[SM, SM] + [VM] * 5,
        out_specs=(VM, VM, VM),
        scratch_shapes=[
            pltpu.VMEM((16, TILE, WIDE), jnp.float32),
            pltpu.VMEM((NY * NZ, TILE, WIDE), jnp.float32),
            pltpu.VMEM((2, 8, HD), jnp.float32),
        ],
        compiler_params=pltpu.CompilerParams(vmem_limit_bytes=VMEM_LIMIT),
    )(pairs, scale, rgbx, cotx, pose, rs, fin)


def output_kernel(
    rgbp, pp, sc,
    rgb_grad, pose_grad, scale_out,
    rbuf, sbuf, fbuf, s_z, s_y, s_t,
    local_sem, r_send, r_recv, z_send, z_recv, f_send, f_recv,
    sz_send, sz_recv, sy_send, sy_recv, st_send, st_recv,
):
    y, z = place()
    t = lax.axis_index("tm")
    greet(
        [((y + k) % NY, z) for k in range(1, NY)] + [(y, (z + k) % NZ) for k in range(1, NZ)],
        [(t + k) % NT for k in range(1, NT)],
    )

    def rgb_copy(k):
        to = (y + k) % NY
        src = rgbp.at[pl.ds(to * 4, 4)]
        dst = rgb_grad.at[:, :, columns(y)]
        if k == 0:
            return pltpu.make_async_copy(src, dst, local_sem.at[0])
        return remote(src, dst, r_send.at[k - 1], r_recv.at[k - 1], to, z)

    def hop(side, step, c, direct):
        to = (z + 1) % NZ if side == 0 else (z + NZ - 1) % NZ
        src = pp.at[goal(side, step) * NY + (y + c) % NY] if direct else sbuf.at[side, step, c]
        return remote(
            src, rbuf.at[side, step, c], z_send.at[side, step, c], z_recv.at[side, step, c], y, to
        )

    def goal(side, step):
        return (z + 4 - step) % NZ if side == 0 else (z + 4 + step) % NZ

    def used(side, step, c):
        return step > 0 or (c < 2) == (side == 0)

    def z_scale(k):
        return remote(sc, s_z.at[z], sz_send.at[k - 1], sz_recv.at[k - 1], y, (z + k) % NZ)

    def y_scale(k):
        ref = s_y.at[y]
        return remote(ref, ref, sy_send.at[k - 1], sy_recv.at[k - 1], (y + k) % NY, z)

    def t_scale(k):
        ref = s_t.at[t]
        return remote_tm(ref, ref, st_send.at[k - 1], st_recv.at[k - 1], (t + k) % NT)

    order = (1, 2, 3, 0)
    sent = []
    for c in order:
        for side in range(2):
            if used(side, 0, c):
                copy = hop(side, 0, c, True)
                copy.start()
                sent.append(copy)
    for k in range(1, NZ):
        z_scale(k).start()
    for k in range(NY):
        rgb_copy(k).start()
    s_z[z] = sc[...]
    for step in range(1, 4):
        for c in order:
            for side in range(2):
                direct = not used(side, step - 1, c)
                if not direct:
                    hop(side, step - 1, c, True).wait_recv()
                    mine = pp[goal(side, step) * NY + (y + c) % NY].astype(jnp.float32)
                    sbuf[side, step, c] = (
                        rbuf[side, step - 1, c].astype(jnp.float32) + mine
                    ).astype(jnp.bfloat16)
                copy = hop(side, step, c, direct)
                copy.start()
                sent.append(copy)
        if step == 1:
            for k in range(1, NZ):
                z_scale(k).wait_recv()
            total = s_z[0]
            for k in range(1, NZ):
                total = total + s_z[k]
            s_y[y] = total
            for k in range(1, NY):
                y_scale(k).start()
        if step == 2:
            for k in range(1, NY):
                y_scale(k).wait_recv()
            row = lax.broadcasted_iota(jnp.int32, (8, HD), 0)
            total = jnp.zeros((8, HD), jnp.float32)
            for k in range(NY):
                for h in range(2):
                    total = jnp.where(row == 2 * k + h, s_y[k, h:h + 1, :], total)
            s_t[t] = total
            for k in range(1, NT):
                t_scale(k).start()

    def final(k):
        to = (y + k) % NY
        src = fbuf.at[k]
        dst = pose_grad.at[:, columns(y)]
        if k == 0:
            return pltpu.make_async_copy(src, dst, local_sem.at[1])
        return remote(src, dst, f_send.at[k - 1], f_recv.at[k - 1], to, z)

    for c in order:
        for side in range(2):
            hop(side, 3, c, False).wait_recv()
        mine = pp[z * NY + (y + c) % NY].astype(jnp.float32)
        fbuf[c] = (
            rbuf[0, 3, c].astype(jnp.float32) + rbuf[1, 3, c].astype(jnp.float32) + mine
        ).astype(jnp.bfloat16)
        final(c).start()
    for k in range(1, NT):
        t_scale(k).wait_recv()
    total = s_t[0]
    for k in range(1, NT):
        total = total + s_t[k]
    scale_out[...] = total
    for k in range(1, NY):
        rgb_copy(k).wait()
        final(k).wait()
        y_scale(k).wait_send()
    rgb_copy(0).wait()
    final(0).wait()
    for k in range(1, NZ):
        z_scale(k).wait_send()
    for k in range(1, NT):
        t_scale(k).wait_send()
    for copy in sent:
        copy.wait_send()


def output(rgbp, pp, sc):
    dma = pltpu.SemaphoreType.DMA
    return pl.pallas_call(
        output_kernel,
        out_shape=(
            jax.ShapeDtypeStruct((4, TILE, 1024), jnp.bfloat16),
            jax.ShapeDtypeStruct((TILE, 1024), jnp.bfloat16),
            jax.ShapeDtypeStruct((8, HD), jnp.float32),
        ),
        in_specs=[ANY, VM, VM],
        out_specs=(ANY, ANY, VM),
        scratch_shapes=[
            pltpu.VMEM((2, 4, NY, TILE, WIDE), jnp.bfloat16),
            pltpu.VMEM((2, 4, NY, TILE, WIDE), jnp.bfloat16),
            pltpu.VMEM((NY, TILE, WIDE), jnp.bfloat16),
            pltpu.VMEM((NZ, 8, HD), jnp.float32),
            pltpu.VMEM((NY, 8, HD), jnp.float32),
            pltpu.VMEM((NT, 8, HD), jnp.float32),
            dma((2,)),
            dma((NY - 1,)), dma((NY - 1,)),
            dma((2, 4, NY)), dma((2, 4, NY)),
            dma((NY - 1,)), dma((NY - 1,)),
            dma((NZ - 1,)), dma((NZ - 1,)),
            dma((NY - 1,)), dma((NY - 1,)),
            dma((NT - 1,)), dma((NT - 1,)),
        ],
        compiler_params=pltpu.CompilerParams(
            collective_id=2, has_side_effects=True, vmem_limit_bytes=VMEM_LIMIT
        ),
    )(rgbp, pp, sc)


def local(rgb_feat, rgb_grad_out, pose_feat, pose_grad_out, logit_scale, pairs):
    y, _ = place()
    scale = lax.dynamic_slice(logit_scale, (2 * y,), (2,))
    rgbx, cotx, pose, codes = gather(
        rgb_feat.reshape(4, TILE, 1024),
        rgb_grad_out.reshape(4, TILE, 1024),
        pose_feat[0],
        pose_grad_out[0],
        pairs,
    )
    st, rs = stats(codes, scale, rgbx, cotx, pose)
    fin = exchange(st)
    rgbp, pp, sc = backward(codes, scale, rgbx, cotx, pose, rs, fin)
    rgb_grad, pose_grad, scale_grad = output(rgbp, pp, sc)
    return rgb_grad.reshape(1, 512, 1024), pose_grad[None], scale_grad[:, 0]


def solution(mesh):
    return jax.shard_map(
        local,
        mesh=mesh,
        in_specs=(
            P("tm", "seq", None),
            P("tm", "seq", None),
            P("tm", "seq", None),
            P("tm", "seq", None),
            P(),
            P("tm", "seq"),
        ),
        out_specs=(P("tm", "seq", None), P("tm", "seq", None), P()),
        check_vma=False,
    )
```

```python
import math

import jax
import jax.numpy as jnp
from jax import lax
from jax.experimental import pallas as pl
from jax.experimental.pallas import tpu as pltpu
from jax.sharding import PartitionSpec as P

NEG = -1e30
NY = 4
NZ = 8
NT = 8
TILE = 128
HD = 128
SLOTS = 5
COUNT = NY * SLOTS
VMEM_LIMIT = 56 * 1024 * 1024
MESH = pl.DeviceIdType.MESH
ANY = pl.BlockSpec(memory_space=pl.ANY)
VM = pl.BlockSpec(memory_space=pltpu.VMEM)
SM = pl.BlockSpec(memory_space=pltpu.SMEM)
POSE, RGB, POSE_KEY, RGB_KEY, POSE_PREV, RGB_PREV, RGB_LAST, POSE_END, RGB_END = range(9)
ORDER = (1, 2, 3, 0)


def place():
    me = lax.axis_index("seq")
    return me // NZ, me % NZ


def remote(src, dst, send_sem, recv_sem, y, z):
    return pltpu.make_async_remote_copy(
        src_ref=src,
        dst_ref=dst,
        send_sem=send_sem,
        recv_sem=recv_sem,
        device_id={"seq": y * NZ + z},
        device_id_type=MESH,
    )


def remote_tm(src, dst, send_sem, recv_sem, t):
    return pltpu.make_async_remote_copy(
        src_ref=src,
        dst_ref=dst,
        send_sem=send_sem,
        recv_sem=recv_sem,
        device_id={"tm": t},
        device_id_type=MESH,
    )


def greet(seqs, tms=()):
    barrier = pltpu.get_barrier_semaphore()
    for y, z in seqs:
        pl.semaphore_signal(
            barrier, inc=1, device_id={"seq": y * NZ + z}, device_id_type=MESH
        )
    for t in tms:
        pl.semaphore_signal(barrier, inc=1, device_id={"tm": t}, device_id_type=MESH)
    pl.semaphore_wait(barrier, len(seqs) + len(tms))


def columns(y, h):
    return pl.ds(pl.multiple_of((2 * y + h) * HD, HD), HD)


def dot_t(a, b):
    return lax.dot_general(a, b, (((1,), (1,)), ((), ())), preferred_element_type=jnp.float32)


def fill_table(codes, tab):
    def slots(n, carry):
        pos = (n // 10) * 2 + n % 2
        code = codes[pos, 0, (n % 10) // 2]
        kept = jnp.maximum(code, 0)
        tile = kept % (NY * NZ)
        pi = (tile % NZ) * NY + tile // NZ
        ri = pos * 4 + kept // (NY * NZ)
        tab[POSE, n] = pi
        tab[RGB, n] = ri
        tab[POSE_KEY, n] = jnp.where(code >= 0, pi, -1 - n)
        tab[RGB_KEY, n] = jnp.where(code >= 0, ri, -1 - n)
        return carry

    lax.fori_loop(0, COUNT, slots, 0)

    def chains(n, carry):
        pose_key, rgb_key = tab[POSE_KEY, n], tab[RGB_KEY, n]
        pose_prev, rgb_prev, rgb_last = COUNT, COUNT, COUNT
        for m in range(COUNT):
            same_rgb = tab[RGB_KEY, m] == rgb_key
            early = n > m
            pose_prev = jnp.where((tab[POSE_KEY, m] == pose_key) & early, m, pose_prev)
            rgb_prev = jnp.where(same_rgb & early, m, rgb_prev)
            rgb_last = jnp.where(same_rgb, m, rgb_last)
        tab[POSE_PREV, n] = pose_prev
        tab[RGB_PREV, n] = rgb_prev
        tab[RGB_LAST, n] = rgb_last
        return carry

    lax.fori_loop(0, COUNT, chains, 0)

    def ends(p, carry):
        pose_end, rgb_end = COUNT, COUNT
        for m in range(COUNT):
            pose_end = jnp.where(tab[POSE_KEY, m] == p, m, pose_end)
            rgb_end = jnp.where(tab[RGB_KEY, m] == p, m, rgb_end)
        tab[POSE_END, p] = pose_end
        tab[RGB_END, p] = rgb_end
        return carry

    lax.fori_loop(0, NY * NZ, ends, 0)


def merge(ref, n, before, high, total, inner):
    old = ref[before, 0:1, :]
    top = jnp.maximum(old, high)
    keep = jnp.exp(old - top)
    add = jnp.exp(high - top)
    ref[n, 0:1, :] = top
    ref[n, 1:2, :] = ref[before, 1:2, :] * keep + total * add
    ref[n, 2:3, :] = ref[before, 2:3, :] * keep + inner * add


def slot_stats(n, tab, factor, rgbx, cotx, pose, st, rs):
    pi, ri = tab[POSE, n], tab[RGB, n]
    q = rgbx[ri]
    g = cotx[ri]
    both = pose[pi].reshape(2 * TILE, HD)
    pf = pose[pi, 0]
    dots = dot_t(q, both)
    score = dots[:, :TILE] * factor
    high = jnp.max(score, axis=0, keepdims=True)
    w = jnp.exp(score - high)
    pose_new = (
        high,
        jnp.sum(w, axis=0, keepdims=True),
        jnp.sum(w * dots[:, TILE:], axis=0, keepdims=True),
    )
    score = dot_t(pf, q) * factor
    grad = dot_t(pf, g)
    high = jnp.max(score, axis=0, keepdims=True)
    w = jnp.exp(score - high)
    rgb_new = (
        high,
        jnp.sum(w, axis=0, keepdims=True),
        jnp.sum(w * grad, axis=0, keepdims=True),
    )
    return pose_new, rgb_new


def slot_backward(n, tab, factor, rgbx, cotx, pose, rs, fin):
    pi, ri = tab[POSE, n], tab[RGB, n]
    last = tab[RGB_LAST, n]
    inverse = 1.0 / jnp.maximum(rs[last, 1:2, :], 1.0)
    rows = jnp.concatenate(
        [rs[last, 0:1, :], inverse, rs[last, 2:3, :] * inverse, jnp.zeros((5, HD), jnp.float32)],
        axis=0,
    )
    rows = jnp.transpose(rows)
    zz, yy = pi // NY, pi % NY
    q = rgbx[ri]
    g = cotx[ri]
    both = pose[pi].reshape(2 * TILE, HD)
    pf = pose[pi, 0]
    pc = pose[pi, 1]
    dots = dot_t(q, both)
    raw = dots[:, :TILE]
    score = raw * factor
    grad = dot_t(g, pf)
    pr = jnp.exp(score - rows[:, 0:1]) * rows[:, 1:2]
    pp = jnp.exp(score - fin[zz, pl.ds(yy, 1), :]) * fin[zz, pl.ds(4 + yy, 1), :]
    ds = pr * (grad - rows[:, 2:3]) + pp * (dots[:, TILE:] - fin[zz, pl.ds(8 + yy, 1), :])
    scale_part = jnp.sum((ds * raw).reshape(TILE // 8, 8, HD), axis=0)
    scale_part = jnp.where(tab[POSE_KEY, n] >= 0, scale_part, 0.0)
    ds_low = ds.astype(jnp.bfloat16)
    pr_low = pr.astype(jnp.bfloat16)
    pp_low = pp.astype(jnp.bfloat16)
    rgb_part = jnp.dot(pp_low, pc, preferred_element_type=jnp.float32) + factor * jnp.dot(
        ds_low, pf, preferred_element_type=jnp.float32
    )
    turned = (((0,), (0,)), ((), ()))
    pose_part = lax.dot_general(
        pr_low, g, turned, preferred_element_type=jnp.float32
    ) + factor * lax.dot_general(ds_low, q, turned, preferred_element_type=jnp.float32)
    return rgb_part, pose_part, scale_part


def fused_kernel(
    rgb_ref, cot_ref, pf_ref, pc_ref, pairs_ref, scale,
    rgb_grad, pose_grad, scale_out, pairs_x,
    rgbx, cotx, pose, st, rs, ex, got, fin, racc, pacc, sacc,
    rgbs, rbuf, sbuf, fbuf, sc, s_z, s_y, s_t, codes, tab,
    own_sem, codes_sem, y_send, y_recv, z_send, z_recv,
    e1_send, e1_recv, e2_send, e2_recv,
    o_own, o_send, o_recv, r_send, r_recv, f_own, f_send, f_recv,
    sz_send, sz_recv, sy_send, sy_recv, st_send, st_recv,
):
    y, z = place()
    t = lax.axis_index("tm")
    sent = []

    def start(copy):
        copy.start()
        sent.append(copy)

    def y_parts(k):
        to = (y + k) % NY
        pos = 3 - k
        parts = [(pairs_ref, pairs_x.at[pos])]
        for h in range(2):
            cols = columns(to, h)
            parts += [
                (pf_ref.at[:, cols], pose[h].at[z * NY + y, 0]),
                (pc_ref.at[:, cols], pose[h].at[z * NY + y, 1]),
                (rgb_ref.at[:, :, cols], rgbx[h].at[pl.ds(pos * 4, 4)]),
                (cot_ref.at[:, :, cols], cotx[h].at[pl.ds(pos * 4, 4)]),
            ]
        return parts

    def own(i):
        src, dst = y_parts(0)[i]
        return pltpu.make_async_copy(src, dst, own_sem.at[i])

    def across(k, i):
        src, dst = y_parts(k)[i]
        return remote(src, dst, y_send.at[k - 1, i], y_recv.at[k - 1, i], (y + k) % NY, z)

    def hop(h, side, step, c):
        block = (z + NZ - step) % NZ if side == 0 else (z + step) % NZ
        to = (z + 1) % NZ if side == 0 else (z + NZ - 1) % NZ
        ref = pose[h].at[block * NY + (y + NY - c) % NY]
        return remote(
            ref, ref, z_send.at[h, side, step, c], z_recv.at[h, side, step, c], y, to
        )

    def last_used(side, c):
        return (c < 2) == (side == 0)

    def ring(h, step):
        for c in range(NY):
            if step == 0:
                for i in (1 + 4 * h, 2 + 4 * h):
                    if c == 0:
                        own(i).wait()
                    else:
                        across(c, i).wait_recv()
            for side in range(2):
                if step > 0:
                    hop(h, side, step - 1, c).wait_recv()
                if step < 3 or last_used(side, c):
                    start(hop(h, side, step, c))

    def ring_end(h):
        for c in range(NY):
            for side in range(2):
                if last_used(side, c):
                    hop(h, side, 3, c).wait_recv()

    def rgb_arrived(h):
        for i in (3 + 4 * h, 4 + 4 * h):
            for k in (1, 2, 3):
                across(k, i).wait_recv()
            own(i).wait()

    factor = [scale[2 * y + h] / math.sqrt(HD) for h in range(2)]

    def stats(h, low, high):
        def body(m, carry):
            news = [
                slot_stats(2 * m + u, tab, factor[h], rgbx[h], cotx[h], pose[h], st[h], rs[h])
                for u in range(2)
            ]
            for u in range(2):
                n = 2 * m + u
                merge(st[h], n, tab[POSE_PREV, n], *news[u][0])
                merge(rs[h], n, tab[RGB_PREV, n], *news[u][1])
            return carry

        lax.fori_loop(low, high, body, 0)

    def backward(h, low, high):
        def body(m, carry):
            news = [
                slot_backward(2 * m + u, tab, factor[h], rgbx[h], cotx[h], pose[h], rs[h], fin[h])
                for u in range(2)
            ]
            for u in range(2):
                n = 2 * m + u
                racc[h][n] = racc[h][tab[RGB_PREV, n]] + news[u][0]
                pacc[h][n] = pacc[h][tab[POSE_PREV, n]] + news[u][1]
            sacc[h] += news[0][2] + news[1][2]
            return carry

        lax.fori_loop(low, high, body, 0)

    def ex_copy(h, k):
        to = (z + k) % NZ
        return remote(
            ex[h].at[to], got[h].at[z], e1_send.at[h, k - 1], e1_recv.at[h, k - 1], y, to
        )

    def fin_copy(h, k):
        ref = fin[h].at[z]
        return remote(ref, ref, e2_send.at[h, k - 1], e2_recv.at[h, k - 1], y, (z + k) % NZ)

    def ex_first(h):
        def pack(zz, carry):
            for yy in range(NY):
                last = tab[POSE_END, zz * NY + yy]
                for i in range(3):
                    ex[h][zz, 4 * i + yy:4 * i + yy + 1, :] = st[h][last, i:i + 1, :]
            return carry

        lax.fori_loop(0, NZ, pack, 0)
        for k in range(1, NZ):
            start(ex_copy(h, k))
        got[h][z] = ex[h][z]

    def ex_second(h):
        for k in range(1, NZ):
            ex_copy(h, k).wait_recv()
        top = got[h][0, 0:4, :]
        for k in range(1, NZ):
            top = jnp.maximum(top, got[h][k, 0:4, :])
        total = jnp.zeros_like(top)
        inner = jnp.zeros_like(top)
        for k in range(NZ):
            keep = jnp.exp(got[h][k, 0:4, :] - top)
            total += got[h][k, 4:8, :] * keep
            inner += got[h][k, 8:12, :] * keep
        inverse = 1.0 / jnp.maximum(total, 1.0)
        fin[h][z, 0:4, :] = top
        fin[h][z, 4:8, :] = inverse
        fin[h][z, 8:12, :] = inner * inverse
        for k in range(1, NZ):
            start(fin_copy(h, k))

    def ex_end(h):
        for k in range(1, NZ):
            fin_copy(h, k).wait_recv()

    def rgb_copy(h, pos):
        src = rgbs[h].at[pos]
        dst = rgb_grad.at[:, :, columns(y, h)]
        if pos == 3:
            return pltpu.make_async_copy(src, dst, o_own.at[h])
        return remote(src, dst, o_send.at[h, pos], o_recv.at[h, pos], (y + 1 + pos) % NY, z)

    def rgb_send(h, pos):
        for i in range(4):
            rgbs[h][pos, i] = racc[h][tab[RGB_END, pos * 4 + i]].astype(jnp.bfloat16)
        rgb_copy(h, pos).start()

    def goal(side, step):
        return (z + 4 - step) % NZ if side == 0 else (z + 4 + step) % NZ

    def back(h, side, step, c):
        to = (z + 1) % NZ if side == 0 else (z + NZ - 1) % NZ
        return remote(
            sbuf[h].at[side, step, c], rbuf[h].at[side, step, c],
            r_send.at[h, side, step, c], r_recv.at[h, side, step, c], y, to,
        )

    def mine(h, block, c):
        return pacc[h][tab[POSE_END, block * NY + (y + c) % NY]]

    def back_step(h, step):
        for c in ORDER:
            for side in range(2):
                if step == 0 and not last_used(side, c):
                    continue
                value = mine(h, goal(side, step), c)
                if step > 1 or (step == 1 and last_used(side, c)):
                    back(h, side, step - 1, c).wait_recv()
                    value = value + rbuf[h][side, step - 1, c].astype(jnp.float32)
                sbuf[h][side, step, c] = value.astype(jnp.bfloat16)
                start(back(h, side, step, c))

    def final(h, c):
        src = fbuf[h].at[c]
        dst = pose_grad.at[:, columns(y, h)]
        if c == 0:
            return pltpu.make_async_copy(src, dst, f_own.at[h])
        return remote(src, dst, f_send.at[h, c - 1], f_recv.at[h, c - 1], (y + c) % NY, z)

    def back_end(h):
        for c in ORDER:
            value = mine(h, z, c)
            for side in range(2):
                back(h, side, 3, c).wait_recv()
                value = value + rbuf[h][side, 3, c].astype(jnp.float32)
            fbuf[h][c] = value.astype(jnp.bfloat16)
            final(h, c).start()

    def z_scale(k):
        return remote(sc, s_z.at[z], sz_send.at[k - 1], sz_recv.at[k - 1], y, (z + k) % NZ)

    def y_scale(k):
        ref = s_y.at[y]
        return remote(ref, ref, sy_send.at[k - 1], sy_recv.at[k - 1], (y + k) % NY, z)

    def t_scale(k):
        ref = s_t.at[t]
        return remote_tm(ref, ref, st_send.at[k - 1], st_recv.at[k - 1], (t + k) % NT)

    def total_of(ref, count):
        total = ref[0]
        for k in range(1, count):
            total = total + ref[k]
        return total

    def scale_first():
        lane = lax.broadcasted_iota(jnp.int32, (8, HD), 1)
        tile = jnp.zeros((8, HD), jnp.float32)
        for h in range(2):
            part = jnp.sum(sacc[h], axis=0, keepdims=True)
            part = jnp.sum(part, axis=1, keepdims=True) / math.sqrt(HD)
            tile = jnp.where(lane == 2 * y + h, part, tile)
        sc[...] = tile
        for k in range(1, NZ):
            start(z_scale(k))
        s_z[z] = tile

    def scale_second():
        for k in range(1, NZ):
            z_scale(k).wait_recv()
        s_y[y] = total_of(s_z, NZ)
        for k in range(1, NY):
            start(y_scale(k))

    def scale_third():
        for k in range(1, NY):
            y_scale(k).wait_recv()
        s_t[t] = total_of(s_y, NY)
        for k in range(1, NT):
            start(t_scale(k))

    def scale_end():
        for k in range(1, NT):
            t_scale(k).wait_recv()
        scale_out[...] = total_of(s_t, NT)

    greet(
        [((y + k) % NY, z) for k in range(1, NY)] + [(y, (z + k) % NZ) for k in range(1, NZ)],
        [(t + k) % NT for k in range(1, NT)],
    )
    for i in (1, 2):
        own(i).start()
    for i in (1, 2, 0, 5, 6):
        for k in (1, 2, 3):
            start(across(k, i))
    for i in (0, 5, 6):
        own(i).start()
    for h in range(2):
        st[h][COUNT, 0:1, :] = jnp.full((1, HD), NEG, jnp.float32)
        rs[h][COUNT, 0:1, :] = jnp.full((1, HD), NEG, jnp.float32)
        st[h][COUNT, 1:3, :] = jnp.zeros((2, HD), jnp.float32)
        rs[h][COUNT, 1:3, :] = jnp.zeros((2, HD), jnp.float32)
        racc[h][COUNT] = jnp.zeros((TILE, HD), jnp.float32)
        pacc[h][COUNT] = jnp.zeros((TILE, HD), jnp.float32)
        sacc[h] = jnp.zeros((8, HD), jnp.float32)
    ring(0, 0)
    for i in (3, 4, 7, 8):
        for k in (1, 2, 3):
            start(across(k, i))
        own(i).start()
    for k in (1, 2, 3):
        across(k, 0).wait_recv()
    own(0).wait()
    to_codes = pltpu.make_async_copy(pairs_x, codes, codes_sem.at[0])
    to_codes.start()
    to_codes.wait()
    ring(0, 1)
    fill_table(codes, tab)
    ring(0, 2)
    ring(0, 3)
    ring(1, 0)
    ring_end(0)
    rgb_arrived(0)
    stats(0, 0, 5)
    ring(1, 1)
    stats(0, 5, 10)
    ex_first(0)
    ring(1, 2)
    ex_second(0)
    ring(1, 3)
    ring_end(1)
    rgb_arrived(1)
    stats(1, 0, 10)
    ex_first(1)
    ex_end(0)
    backward(0, 0, 5)
    rgb_send(0, 0)
    rgb_send(0, 1)
    ex_second(1)
    backward(0, 5, 10)
    rgb_send(0, 2)
    rgb_send(0, 3)
    back_step(0, 0)
    ex_end(1)
    backward(1, 0, 5)
    rgb_send(1, 0)
    rgb_send(1, 1)
    back_step(0, 1)
    backward(1, 5, 10)
    back_step(1, 0)
    rgb_send(1, 2)
    rgb_send(1, 3)
    back_step(0, 2)
    scale_first()
    back_step(1, 1)
    back_step(0, 3)
    scale_second()
    back_step(1, 2)
    back_end(0)
    scale_third()
    back_step(1, 3)
    back_end(1)
    scale_end()
    for h in range(2):
        for pos in range(4):
            rgb_copy(h, pos).wait()
        for c in range(NY):
            final(h, c).wait()
    for copy in sent:
        copy.wait_send()


def fused(rgb, cot, pf, pc, pairs, scale):
    dma = pltpu.SemaphoreType.DMA
    low, full = jnp.bfloat16, jnp.float32

    def twice(shape, kind):
        return [pltpu.VMEM(shape, kind)] * 2

    return pl.pallas_call(
        fused_kernel,
        out_shape=(
            jax.ShapeDtypeStruct((4, TILE, 1024), low),
            jax.ShapeDtypeStruct((TILE, 1024), low),
            jax.ShapeDtypeStruct((8, HD), full),
            jax.ShapeDtypeStruct((NY, 1, SLOTS), jnp.int32),
        ),
        in_specs=[ANY] * 5 + [SM],
        out_specs=(ANY, ANY, VM, ANY),
        scratch_shapes=[
            twice((16, TILE, HD), low),
            twice((16, TILE, HD), low),
            twice((NY * NZ, 2, TILE, HD), low),
            twice((COUNT + 1, 8, HD), full),
            twice((COUNT + 1, 8, HD), full),
            twice((NZ, 16, HD), full),
            twice((NZ, 16, HD), full),
            twice((NZ, 16, HD), full),
            twice((COUNT + 1, TILE, HD), full),
            twice((COUNT + 1, TILE, HD), full),
            pltpu.VMEM((2, 8, HD), full),
            twice((4, 4, TILE, HD), low),
            twice((2, 4, NY, TILE, HD), low),
            twice((2, 4, NY, TILE, HD), low),
            twice((NY, TILE, HD), low),
            pltpu.VMEM((8, HD), full),
            pltpu.VMEM((NZ, 8, HD), full),
            pltpu.VMEM((NY, 8, HD), full),
            pltpu.VMEM((NT, 8, HD), full),
            pltpu.SMEM((NY, 1, SLOTS), jnp.int32),
            pltpu.SMEM((9, NY * NZ), jnp.int32),
            dma((9,)), dma((1,)), dma((3, 9)), dma((3, 9)),
            dma((2, 2, 4, NY)), dma((2, 2, 4, NY)),
            dma((2, NZ - 1)), dma((2, NZ - 1)), dma((2, NZ - 1)), dma((2, NZ - 1)),
            dma((2,)), dma((2, 3)), dma((2, 3)),
            dma((2, 2, 4, NY)), dma((2, 2, 4, NY)),
            dma((2,)), dma((2, 3)), dma((2, 3)),
            dma((NZ - 1,)), dma((NZ - 1,)),
            dma((NY - 1,)), dma((NY - 1,)),
            dma((NT - 1,)), dma((NT - 1,)),
        ],
        compiler_params=pltpu.CompilerParams(
            collective_id=0, has_side_effects=True, vmem_limit_bytes=VMEM_LIMIT
        ),
    )(rgb, cot, pf, pc, pairs, scale)


def local(rgb_feat, rgb_grad_out, pose_feat, pose_grad_out, logit_scale, pairs):
    rgb_grad, pose_grad, scale_grad, _ = fused(
        rgb_feat.reshape(4, TILE, 1024),
        rgb_grad_out.reshape(4, TILE, 1024),
        pose_feat[0],
        pose_grad_out[0],
        pairs,
        logit_scale,
    )
    return rgb_grad.reshape(1, 512, 1024), pose_grad[None], scale_grad[0, :8]


def solution(mesh):
    return jax.shard_map(
        local,
        mesh=mesh,
        in_specs=(
            P("tm", "seq", None),
            P("tm", "seq", None),
            P("tm", "seq", None),
            P("tm", "seq", None),
            P(),
            P("tm", "seq"),
        ),
        out_specs=(P("tm", "seq", None), P("tm", "seq", None), P()),
        check_vma=False,
    )
```

```python
import math

import jax
import jax.numpy as jnp
from jax import lax
from jax.experimental import pallas as pl
from jax.experimental.pallas import tpu as pltpu
from jax.sharding import PartitionSpec as P

NEG = -1e30
NY = 4
NZ = 8
NT = 8
TILE = 128
HD = 128
SLOTS = 5
COUNT = NY * SLOTS
VMEM_LIMIT = 56 * 1024 * 1024
MESH = pl.DeviceIdType.MESH
ANY = pl.BlockSpec(memory_space=pl.ANY)
VM = pl.BlockSpec(memory_space=pltpu.VMEM)
SM = pl.BlockSpec(memory_space=pltpu.SMEM)
POSE, RGB, POSE_KEY, RGB_KEY, POSE_PREV, RGB_PREV, RGB_LAST, POSE_END, RGB_END = range(9)
ORDER = (1, 2, 3, 0)
CHUNKS = (0, 1, 3, 2)
STATS_UNROLL = 10
UNROLL = 5


def place():
    me = lax.axis_index("seq")
    return me // NZ, me % NZ


def remote(src, dst, send_sem, recv_sem, y, z):
    return pltpu.make_async_remote_copy(
        src_ref=src,
        dst_ref=dst,
        send_sem=send_sem,
        recv_sem=recv_sem,
        device_id={"seq": y * NZ + z},
        device_id_type=MESH,
    )


def remote_tm(src, dst, send_sem, recv_sem, t):
    return pltpu.make_async_remote_copy(
        src_ref=src,
        dst_ref=dst,
        send_sem=send_sem,
        recv_sem=recv_sem,
        device_id={"tm": t},
        device_id_type=MESH,
    )


def greet(seqs, tms=()):
    barrier = pltpu.get_barrier_semaphore()
    for y, z in seqs:
        pl.semaphore_signal(
            barrier, inc=1, device_id={"seq": y * NZ + z}, device_id_type=MESH
        )
    for t in tms:
        pl.semaphore_signal(barrier, inc=1, device_id={"tm": t}, device_id_type=MESH)
    pl.semaphore_wait(barrier, len(seqs) + len(tms))


def columns(y, h):
    return pl.ds(pl.multiple_of((2 * y + h) * HD, HD), HD)


def dot_t(a, b):
    return lax.dot_general(a, b, (((1,), (1,)), ((), ())), preferred_element_type=jnp.float32)


def fill_table(codes, tab):
    def slots(n, carry):
        pos = (n // 10) * 2 + n % 2
        code = codes[pos, 0, (n % 10) // 2]
        kept = jnp.maximum(code, 0)
        tile = kept % (NY * NZ)
        pi = (tile % NZ) * NY + tile // NZ
        ri = pos * 4 + kept // (NY * NZ)
        tab[POSE, n] = pi
        tab[RGB, n] = ri
        tab[POSE_KEY, n] = jnp.where(code >= 0, pi, -1 - n)
        tab[RGB_KEY, n] = jnp.where(code >= 0, ri, -1 - n)
        return carry

    lax.fori_loop(0, COUNT, slots, 0)

    def chains(n, carry):
        pose_key, rgb_key = tab[POSE_KEY, n], tab[RGB_KEY, n]
        pose_prev, rgb_prev, rgb_last = COUNT, COUNT, COUNT
        for m in range(COUNT):
            same_rgb = tab[RGB_KEY, m] == rgb_key
            early = n > m
            pose_prev = jnp.where((tab[POSE_KEY, m] == pose_key) & early, m, pose_prev)
            rgb_prev = jnp.where(same_rgb & early, m, rgb_prev)
            rgb_last = jnp.where(same_rgb, m, rgb_last)
        tab[POSE_PREV, n] = pose_prev
        tab[RGB_PREV, n] = rgb_prev
        tab[RGB_LAST, n] = rgb_last
        return carry

    lax.fori_loop(0, COUNT, chains, 0)

    def ends(p, carry):
        pose_end, rgb_end = COUNT, COUNT
        for m in range(COUNT):
            pose_end = jnp.where(tab[POSE_KEY, m] == p, m, pose_end)
            rgb_end = jnp.where(tab[RGB_KEY, m] == p, m, rgb_end)
        tab[POSE_END, p] = pose_end
        tab[RGB_END, p] = rgb_end
        return carry

    lax.fori_loop(0, NY * NZ, ends, 0)


def merge(ref, n, before, high, total, inner):
    old = ref[before, 0:1, :]
    top = jnp.maximum(old, high)
    keep = jnp.exp(old - top)
    add = jnp.exp(high - top)
    ref[n, 0:1, :] = top
    ref[n, 1:2, :] = ref[before, 1:2, :] * keep + total * add
    ref[n, 2:3, :] = ref[before, 2:3, :] * keep + inner * add


def slot_stats(n, tab, factor, qg, pose):
    pi, ri = tab[POSE, n], tab[RGB, n]
    q = qg[ri, 0]
    g = qg[ri, 1]
    both = pose[pi].reshape(2 * TILE, HD)
    pf = pose[pi, 0]
    dots = dot_t(q, both)
    score = dots[:, :TILE] * factor
    high = jnp.max(score, axis=0, keepdims=True)
    w = jnp.exp(score - high)
    pose_new = (
        high,
        jnp.sum(w, axis=0, keepdims=True),
        jnp.sum(w * dots[:, TILE:], axis=0, keepdims=True),
    )
    dots = dot_t(pf, qg[ri].reshape(2 * TILE, HD))
    score = dots[:, :TILE] * factor
    high = jnp.max(score, axis=0, keepdims=True)
    w = jnp.exp(score - high)
    rgb_new = (
        high,
        jnp.sum(w, axis=0, keepdims=True),
        jnp.sum(w * dots[:, TILE:], axis=0, keepdims=True),
    )
    return pose_new, rgb_new


TURNED = (((0,), (0,)), ((), ()))


def slot_before(n, tab, factor, qg, pose, rs):
    pi, ri = tab[POSE, n], tab[RGB, n]
    last = tab[RGB_LAST, n]
    inverse = 1.0 / jnp.maximum(rs[last, 1:2, :], 1.0)
    rows = jnp.concatenate(
        [rs[last, 0:1, :], inverse, rs[last, 2:3, :] * inverse, jnp.zeros((5, HD), jnp.float32)],
        axis=0,
    )
    rows = jnp.transpose(rows)
    q = qg[ri, 0]
    g = qg[ri, 1]
    both = pose[pi].reshape(2 * TILE, HD)
    dots = dot_t(q, both)
    score = dots[:, :TILE] * factor
    grad = dot_t(g, pose[pi, 0])
    pr = jnp.exp(score - rows[:, 0:1]) * rows[:, 1:2]
    own = pr * (grad - rows[:, 2:3])
    part = lax.dot_general(
        pr.astype(jnp.bfloat16), g, TURNED, preferred_element_type=jnp.float32
    )
    return score, own, dots[:, TILE:], part


def slot_after(n, tab, factor, qg, pose, fin, keep):
    pi, ri = tab[POSE, n], tab[RGB, n]
    zz, yy = pi // NY, pi % NY
    score = keep[0, n]
    pp = jnp.exp(score - fin[zz, pl.ds(yy, 1), :]) * fin[zz, pl.ds(4 + yy, 1), :]
    ds = keep[1, n] + pp * (keep[2, n] - fin[zz, pl.ds(8 + yy, 1), :])
    scale_part = jnp.sum((ds * score).reshape(TILE // 8, 8, HD), axis=0)
    scale_part = jnp.where(tab[POSE_KEY, n] >= 0, scale_part, 0.0)
    ds_low = (ds * factor).astype(jnp.bfloat16)
    pair = jnp.concatenate([ds_low, pp.astype(jnp.bfloat16)], axis=1)
    rgb_part = jnp.dot(
        pair, pose[pi].reshape(2 * TILE, HD), preferred_element_type=jnp.float32
    )
    pose_part = lax.dot_general(ds_low, qg[ri, 0], TURNED, preferred_element_type=jnp.float32)
    return rgb_part, pose_part, scale_part


def fused_kernel(
    rgb_ref, cot_ref, pf_ref, pc_ref, pairs_ref, scale,
    rgb_grad, pose_grad, scale_out, pairs_x,
    qg, pose, st, rs, keep, ex, got, fin, racc, pacc, sacc,
    rgbs, rbuf, sbuf, fbuf, sc, s_z, s_y, s_t, codes, tab,
    own_sem, codes_sem, y_send, y_recv, z_send, z_recv, b_send, b_recv,
    e1_send, e1_recv, e2_send, e2_recv,
    o_own, o_send, o_recv, r_send, r_recv, f_own, f_send, f_recv,
    sz_send, sz_recv, sy_send, sy_recv, st_send, st_recv,
):
    y, z = place()
    t = lax.axis_index("tm")
    sent = []

    def start(copy):
        copy.start()
        sent.append(copy)

    def y_parts(k):
        to = (y + k) % NY
        pos = 3 - k
        parts = [(pairs_ref, pairs_x.at[pos])]
        for h in range(2):
            cols = columns(to, h)
            parts += [
                (pf_ref.at[:, cols], pose[h].at[z * NY + y, 0]),
                (pc_ref.at[:, cols], pose[h].at[z * NY + y, 1]),
                (rgb_ref.at[:, :, cols], qg[h].at[pl.ds(pos * 4, 4), 0]),
                (cot_ref.at[:, :, cols], qg[h].at[pl.ds(pos * 4, 4), 1]),
            ]
        return parts

    def own(i):
        src, dst = y_parts(0)[i]
        return pltpu.make_async_copy(src, dst, own_sem.at[i])

    def across(k, i):
        src, dst = y_parts(k)[i]
        return remote(src, dst, y_send.at[k - 1, i], y_recv.at[k - 1, i], (y + k) % NY, z)

    def hop(h, side, step, c):
        block = (z + NZ - step) % NZ if side == 0 else (z + step) % NZ
        to = (z + 1) % NZ if side == 0 else (z + NZ - 1) % NZ
        ref = pose[h].at[block * NY + (y + NY - c) % NY]
        return remote(
            ref, ref, z_send.at[h, side, step, c], z_recv.at[h, side, step, c], y, to
        )

    def last_used(side, c):
        return (c < 2) == (side == 0)

    def begin(h, side, i):
        src, dst = y_parts(0)[1 + 4 * h + i]
        to = (z + 1) % NZ if side == 0 else (z + NZ - 1) % NZ
        return remote(src, dst, b_send.at[h, side, i], b_recv.at[h, side, i], y, to)

    def ring(h, step, c):
        if step == 0:
            across(c, 1 + 4 * h).wait_recv()
            across(c, 2 + 4 * h).wait_recv()
        for side in range(2):
            if step == 1 and c == 0:
                begin(h, side, 0).wait_recv()
                begin(h, side, 1).wait_recv()
            elif step > 0:
                hop(h, side, step - 1, c).wait_recv()
            if step < 3 or last_used(side, c):
                start(hop(h, side, step, c))

    def ring_all(h, step):
        for c in CHUNKS:
            ring(h, step, c)

    def ring_end(h):
        for c in range(NY):
            for side in range(2):
                if last_used(side, c):
                    hop(h, side, 3, c).wait_recv()

    def rgb_arrived(h):
        own(1 + 4 * h).wait()
        own(2 + 4 * h).wait()
        for i in (3 + 4 * h, 4 + 4 * h):
            for k in (1, 2, 3):
                across(k, i).wait_recv()
            own(i).wait()

    factor = [scale[2 * y + h] / math.sqrt(HD) for h in range(2)]

    def stats(h):
        def body(m, carry):
            slots = [STATS_UNROLL * m + u for u in range(STATS_UNROLL)]
            news = [slot_stats(n, tab, factor[h], qg[h], pose[h]) for n in slots]
            for n, (pose_new, rgb_new) in zip(slots, news):
                merge(st[h], n, tab[POSE_PREV, n], *pose_new)
                merge(rs[h], n, tab[RGB_PREV, n], *rgb_new)
            return carry

        lax.fori_loop(0, COUNT // STATS_UNROLL, body, 0)

    def before(h, low, high):
        def body(m, carry):
            slots = [UNROLL * m + u for u in range(UNROLL)]
            news = [slot_before(n, tab, factor[h], qg[h], pose[h], rs[h]) for n in slots]
            for n, new in zip(slots, news):
                for i in range(3):
                    keep[i, n] = new[i]
                pacc[h][n] = new[3]
            return carry

        lax.fori_loop(low, high, body, 0)

    def after(h, low, high):
        def body(m, carry):
            slots = [UNROLL * m + u for u in range(UNROLL)]
            news = [slot_after(n, tab, factor[h], qg[h], pose[h], fin[h], keep) for n in slots]
            for n, new in zip(slots, news):
                racc[h][n] = racc[h][tab[RGB_PREV, n]] + new[0]
                pacc[h][n] = pacc[h][tab[POSE_PREV, n]] + (pacc[h][n] + new[1])
            sacc[h] += sum(new[2] for new in news)
            return carry

        lax.fori_loop(low, high, body, 0)

    def ex_copy(h, k):
        to = (z + k) % NZ
        return remote(
            ex[h].at[to], got[h].at[z], e1_send.at[h, k - 1], e1_recv.at[h, k - 1], y, to
        )

    def fin_copy(h, k):
        ref = fin[h].at[z]
        return remote(ref, ref, e2_send.at[h, k - 1], e2_recv.at[h, k - 1], y, (z + k) % NZ)

    def ex_first(h):
        def pack(zz, carry):
            for yy in range(NY):
                last = tab[POSE_END, zz * NY + yy]
                for i in range(3):
                    ex[h][zz, 4 * i + yy:4 * i + yy + 1, :] = st[h][last, i:i + 1, :]
            return carry

        lax.fori_loop(0, NZ, pack, 0)
        for k in range(1, NZ):
            start(ex_copy(h, k))
        got[h][z] = ex[h][z]

    def ex_second(h):
        for k in range(1, NZ):
            ex_copy(h, k).wait_recv()
        top = got[h][0, 0:4, :]
        for k in range(1, NZ):
            top = jnp.maximum(top, got[h][k, 0:4, :])
        total = jnp.zeros_like(top)
        inner = jnp.zeros_like(top)
        for k in range(NZ):
            keep = jnp.exp(got[h][k, 0:4, :] - top)
            total += got[h][k, 4:8, :] * keep
            inner += got[h][k, 8:12, :] * keep
        inverse = 1.0 / jnp.maximum(total, 1.0)
        fin[h][z, 0:4, :] = top
        fin[h][z, 4:8, :] = inverse
        fin[h][z, 8:12, :] = inner * inverse
        for k in range(1, NZ):
            start(fin_copy(h, k))

    def ex_end(h):
        for k in range(1, NZ):
            fin_copy(h, k).wait_recv()

    def rgb_copy(h, pos):
        src = rgbs[h].at[pos]
        dst = rgb_grad.at[:, :, columns(y, h)]
        if pos == 3:
            return pltpu.make_async_copy(src, dst, o_own.at[h])
        return remote(src, dst, o_send.at[h, pos], o_recv.at[h, pos], (y + 1 + pos) % NY, z)

    def rgb_send(h, pos):
        for i in range(4):
            rgbs[h][pos, i] = racc[h][tab[RGB_END, pos * 4 + i]].astype(jnp.bfloat16)
        rgb_copy(h, pos).start()

    def goal(side, step):
        return (z + 4 - step) % NZ if side == 0 else (z + 4 + step) % NZ

    def back(h, side, step, c):
        to = (z + 1) % NZ if side == 0 else (z + NZ - 1) % NZ
        return remote(
            sbuf[h].at[side, step, c], rbuf[h].at[side, step, c],
            r_send.at[h, side, step, c], r_recv.at[h, side, step, c], y, to,
        )

    def mine(h, block, c):
        return pacc[h][tab[POSE_END, block * NY + (y + c) % NY]]

    def back_step(h, step):
        for c in ORDER:
            for side in range(2):
                if step == 0 and not last_used(side, c):
                    continue
                value = mine(h, goal(side, step), c)
                if step > 1 or (step == 1 and last_used(side, c)):
                    back(h, side, step - 1, c).wait_recv()
                    value = value + rbuf[h][side, step - 1, c].astype(jnp.float32)
                sbuf[h][side, step, c] = value.astype(jnp.bfloat16)
                start(back(h, side, step, c))

    def final(h, c):
        src = fbuf[h].at[c]
        dst = pose_grad.at[:, columns(y, h)]
        if c == 0:
            return pltpu.make_async_copy(src, dst, f_own.at[h])
        return remote(src, dst, f_send.at[h, c - 1], f_recv.at[h, c - 1], (y + c) % NY, z)

    def back_end(h):
        for c in ORDER:
            value = mine(h, z, c)
            for side in range(2):
                back(h, side, 3, c).wait_recv()
                value = value + rbuf[h][side, 3, c].astype(jnp.float32)
            fbuf[h][c] = value.astype(jnp.bfloat16)
            final(h, c).start()

    def z_scale(k):
        return remote(sc, s_z.at[z], sz_send.at[k - 1], sz_recv.at[k - 1], y, (z + k) % NZ)

    def y_scale(k):
        ref = s_y.at[y]
        return remote(ref, ref, sy_send.at[k - 1], sy_recv.at[k - 1], (y + k) % NY, z)

    def t_scale(k):
        ref = s_t.at[t]
        return remote_tm(ref, ref, st_send.at[k - 1], st_recv.at[k - 1], (t + k) % NT)

    def total_of(ref, count):
        total = ref[0]
        for k in range(1, count):
            total = total + ref[k]
        return total

    def scale_first():
        lane = lax.broadcasted_iota(jnp.int32, (8, HD), 1)
        tile = jnp.zeros((8, HD), jnp.float32)
        for h in range(2):
            part = jnp.sum(sacc[h], axis=0, keepdims=True)
            part = jnp.sum(part, axis=1, keepdims=True) / scale[2 * y + h]
            tile = jnp.where(lane == 2 * y + h, part, tile)
        sc[...] = tile
        for k in range(1, NZ):
            start(z_scale(k))
        s_z[z] = tile

    def scale_second():
        for k in range(1, NZ):
            z_scale(k).wait_recv()
        s_y[y] = total_of(s_z, NZ)
        for k in range(1, NY):
            start(y_scale(k))

    def scale_third():
        for k in range(1, NY):
            y_scale(k).wait_recv()
        s_t[t] = total_of(s_y, NY)
        for k in range(1, NT):
            start(t_scale(k))

    def scale_end():
        for k in range(1, NT):
            t_scale(k).wait_recv()
        scale_out[...] = total_of(s_t, NT)

    greet(
        [((y + k) % NY, z) for k in range(1, NY)] + [(y, (z + k) % NZ) for k in range(1, NZ)],
        [(t + k) % NT for k in range(1, NT)],
    )
    for h in range(2):
        for i in range(2):
            for side in range(2):
                start(begin(h, side, i))
        for i in (1 + 4 * h, 2 + 4 * h):
            for k in (1, 2, 3):
                start(across(k, i))
    for k in (1, 2, 3):
        start(across(k, 0))
    for i in (0, 1, 2, 5, 6):
        own(i).start()
    for h in range(2):
        st[h][COUNT, 0:1, :] = jnp.full((1, HD), NEG, jnp.float32)
        rs[h][COUNT, 0:1, :] = jnp.full((1, HD), NEG, jnp.float32)
        st[h][COUNT, 1:3, :] = jnp.zeros((2, HD), jnp.float32)
        rs[h][COUNT, 1:3, :] = jnp.zeros((2, HD), jnp.float32)
        racc[h][COUNT] = jnp.zeros((TILE, HD), jnp.float32)
        pacc[h][COUNT] = jnp.zeros((TILE, HD), jnp.float32)
        sacc[h] = jnp.zeros((8, HD), jnp.float32)
    for c in CHUNKS[1:]:
        ring(0, 0, c)
    for i in (3, 4, 7, 8):
        for k in (1, 2, 3):
            start(across(k, i))
        own(i).start()
    for k in (1, 2, 3):
        across(k, 0).wait_recv()
    own(0).wait()
    to_codes = pltpu.make_async_copy(pairs_x, codes, codes_sem.at[0])
    to_codes.start()
    to_codes.wait()
    ring_all(0, 1)
    fill_table(codes, tab)
    ring_all(0, 2)
    ring_all(0, 3)
    for c in CHUNKS[1:]:
        ring(1, 0, c)
    ring_end(0)
    ring_all(1, 1)
    rgb_arrived(0)
    stats(0)
    ex_first(0)
    ring(1, 2, CHUNKS[0])
    ring(1, 2, CHUNKS[1])
    before(0, 0, 1)
    ring(1, 2, CHUNKS[2])
    before(0, 1, 2)
    ring(1, 2, CHUNKS[3])
    before(0, 2, 3)
    ex_second(0)
    ring(1, 3, CHUNKS[0])
    before(0, 3, 4)
    for c in CHUNKS[1:]:
        ring(1, 3, c)
    ex_end(0)
    after(0, 0, 4)
    back_step(0, 0)
    for pos in range(4):
        rgb_send(0, pos)
    ring_end(1)
    rgb_arrived(1)
    stats(1)
    ex_first(1)
    back_step(0, 1)
    before(1, 0, 2)
    back_step(0, 2)
    ex_second(1)
    before(1, 2, 4)
    back_step(0, 3)
    ex_end(1)
    after(1, 0, 4)
    back_step(1, 0)
    for pos in range(4):
        rgb_send(1, pos)
    scale_first()
    back_end(0)
    back_step(1, 1)
    scale_second()
    back_step(1, 2)
    scale_third()
    back_step(1, 3)
    back_end(1)
    scale_end()
    for h in range(2):
        for pos in range(4):
            rgb_copy(h, pos).wait()
        for c in range(NY):
            final(h, c).wait()
    for copy in sent:
        copy.wait_send()


def fused(rgb, cot, pf, pc, pairs, scale):
    dma = pltpu.SemaphoreType.DMA
    low, full = jnp.bfloat16, jnp.float32

    def twice(shape, kind):
        return [pltpu.VMEM(shape, kind)] * 2

    return pl.pallas_call(
        fused_kernel,
        out_shape=(
            jax.ShapeDtypeStruct((4, TILE, 1024), low),
            jax.ShapeDtypeStruct((TILE, 1024), low),
            jax.ShapeDtypeStruct((8, HD), full),
            jax.ShapeDtypeStruct((NY, 1, SLOTS), jnp.int32),
        ),
        in_specs=[ANY] * 5 + [SM],
        out_specs=(ANY, ANY, VM, ANY),
        scratch_shapes=[
            twice((16, 2, TILE, HD), low),
            twice((NY * NZ, 2, TILE, HD), low),
            twice((COUNT + 1, 8, HD), full),
            twice((COUNT + 1, 8, HD), full),
            pltpu.VMEM((3, COUNT, TILE, HD), full),
            twice((NZ, 16, HD), full),
            twice((NZ, 16, HD), full),
            twice((NZ, 16, HD), full),
            twice((COUNT + 1, TILE, HD), full),
            twice((COUNT + 1, TILE, HD), full),
            pltpu.VMEM((2, 8, HD), full),
            twice((4, 4, TILE, HD), low),
            twice((2, 4, NY, TILE, HD), low),
            twice((2, 4, NY, TILE, HD), low),
            twice((NY, TILE, HD), low),
            pltpu.VMEM((8, HD), full),
            pltpu.VMEM((NZ, 8, HD), full),
            pltpu.VMEM((NY, 8, HD), full),
            pltpu.VMEM((NT, 8, HD), full),
            pltpu.SMEM((NY, 1, SLOTS), jnp.int32),
            pltpu.SMEM((9, NY * NZ), jnp.int32),
            dma((9,)), dma((1,)), dma((3, 9)), dma((3, 9)),
            dma((2, 2, 4, NY)), dma((2, 2, 4, NY)), dma((2, 2, 2)), dma((2, 2, 2)),
            dma((2, NZ - 1)), dma((2, NZ - 1)), dma((2, NZ - 1)), dma((2, NZ - 1)),
            dma((2,)), dma((2, 3)), dma((2, 3)),
            dma((2, 2, 4, NY)), dma((2, 2, 4, NY)),
            dma((2,)), dma((2, 3)), dma((2, 3)),
            dma((NZ - 1,)), dma((NZ - 1,)),
            dma((NY - 1,)), dma((NY - 1,)),
            dma((NT - 1,)), dma((NT - 1,)),
        ],
        compiler_params=pltpu.CompilerParams(
            collective_id=0, has_side_effects=True, vmem_limit_bytes=VMEM_LIMIT
        ),
    )(rgb, cot, pf, pc, pairs, scale)


def finish_kernel(rgb, pose, scale, rgb_out, pose_out, scale_out, rgb_held, pose_held, sem):
    steps = [
        (rgb.at[i], rgb_held.at[i], rgb_out.at[i]) for i in range(4)
    ] + [(pose, pose_held, pose_out)]
    ins = [
        pltpu.make_async_copy(src, held, sem.at[0, i]) for i, (src, held, _) in enumerate(steps)
    ]
    outs = [
        pltpu.make_async_copy(held, dst, sem.at[1, i]) for i, (_, held, dst) in enumerate(steps)
    ]
    for copy in ins:
        copy.start()
    scale_out[...] = scale[0:1, 0:8]
    for arrive, leave in zip(ins, outs):
        arrive.wait()
        leave.start()
    for copy in outs:
        copy.wait()


def finish(rgb, pose, scale):
    return pl.pallas_call(
        finish_kernel,
        out_shape=(
            jax.ShapeDtypeStruct(rgb.shape, rgb.dtype),
            jax.ShapeDtypeStruct(pose.shape, pose.dtype),
            jax.ShapeDtypeStruct((1, 8), jnp.float32),
        ),
        in_specs=[ANY, ANY, VM],
        out_specs=(ANY, ANY, VM),
        scratch_shapes=[
            pltpu.VMEM(rgb.shape, rgb.dtype),
            pltpu.VMEM(pose.shape, pose.dtype),
            pltpu.SemaphoreType.DMA((2, 5)),
        ],
        compiler_params=pltpu.CompilerParams(vmem_limit_bytes=VMEM_LIMIT),
    )(rgb, pose, scale)


def local(rgb_feat, rgb_grad_out, pose_feat, pose_grad_out, logit_scale, pairs):
    rgb_grad, pose_grad, scale_grad, _ = fused(
        rgb_feat.reshape(4, TILE, 1024),
        rgb_grad_out.reshape(4, TILE, 1024),
        pose_feat[0],
        pose_grad_out[0],
        pairs,
        logit_scale,
    )
    rgb_grad, pose_grad, scale_grad = finish(rgb_grad, pose_grad, scale_grad)
    return rgb_grad.reshape(1, 512, 1024), pose_grad[None], scale_grad[0]


def solution(mesh):
    return jax.shard_map(
        local,
        mesh=mesh,
        in_specs=(
            P("tm", "seq", None),
            P("tm", "seq", None),
            P("tm", "seq", None),
            P("tm", "seq", None),
            P(),
            P("tm", "seq"),
        ),
        out_specs=(P("tm", "seq", None), P("tm", "seq", None), P()),
        check_vma=False,
    )
```

```python
import math

import jax
import jax.numpy as jnp
from jax import lax
from jax.experimental import pallas as pl
from jax.experimental.pallas import tpu as pltpu
from jax.sharding import PartitionSpec as P

NEG = -1e30
NY = 4
NZ = 8
NT = 8
TILE = 128
HD = 128
SLOTS = 5
COUNT = NY * SLOTS
VMEM_LIMIT = 28 * 1024 * 1024
MESH = pl.DeviceIdType.MESH
ANY = pl.BlockSpec(memory_space=pl.ANY)
HBM = pl.BlockSpec(memory_space=pltpu.HBM)
VM = pl.BlockSpec(memory_space=pltpu.VMEM)
SM = pl.BlockSpec(memory_space=pltpu.SMEM)
POSE, RGB, POSE_KEY, RGB_KEY, POSE_PREV, RGB_PREV, RGB_LAST, POSE_END, RGB_END = range(9)
CHUNKS = (0, 1, 3, 2)
STATS_UNROLL = 10
UNROLL = 5


def place():
    me = lax.axis_index("seq")
    return me // NZ, me % NZ


def remote(src, dst, send_sem, recv_sem, y, z):
    return pltpu.make_async_remote_copy(
        src_ref=src,
        dst_ref=dst,
        send_sem=send_sem,
        recv_sem=recv_sem,
        device_id={"seq": y * NZ + z},
        device_id_type=MESH,
    )


def remote_tm(src, dst, send_sem, recv_sem, t):
    return pltpu.make_async_remote_copy(
        src_ref=src,
        dst_ref=dst,
        send_sem=send_sem,
        recv_sem=recv_sem,
        device_id={"tm": t},
        device_id_type=MESH,
    )


def greet(seqs, tms=()):
    barrier = pltpu.get_barrier_semaphore()
    for y, z in seqs:
        pl.semaphore_signal(
            barrier, inc=1, device_id={"seq": y * NZ + z}, device_id_type=MESH
        )
    for t in tms:
        pl.semaphore_signal(barrier, inc=1, device_id={"tm": t}, device_id_type=MESH)
    pl.semaphore_wait(barrier, len(seqs) + len(tms))


def columns(y, h):
    return pl.ds(pl.multiple_of((2 * y + h) * HD, HD), HD)


def dot_t(a, b):
    return lax.dot_general(a, b, (((1,), (1,)), ((), ())), preferred_element_type=jnp.float32)


def fill_table(codes, tab):
    def slots(n, carry):
        pos = (n // 10) * 2 + n % 2
        code = codes[pos, 0, (n % 10) // 2]
        kept = jnp.maximum(code, 0)
        tile = kept % (NY * NZ)
        pi = (tile % NZ) * NY + tile // NZ
        ri = pos * 4 + kept // (NY * NZ)
        tab[POSE, n] = pi
        tab[RGB, n] = ri
        tab[POSE_KEY, n] = jnp.where(code >= 0, pi, -1 - n)
        tab[RGB_KEY, n] = jnp.where(code >= 0, ri, -1 - n)
        return carry

    lax.fori_loop(0, COUNT, slots, 0)

    def chains(n, carry):
        pose_key, rgb_key = tab[POSE_KEY, n], tab[RGB_KEY, n]
        pose_prev, rgb_prev, rgb_last = COUNT, COUNT, COUNT
        for m in range(COUNT):
            same_rgb = tab[RGB_KEY, m] == rgb_key
            early = n > m
            pose_prev = jnp.where((tab[POSE_KEY, m] == pose_key) & early, m, pose_prev)
            rgb_prev = jnp.where(same_rgb & early, m, rgb_prev)
            rgb_last = jnp.where(same_rgb, m, rgb_last)
        tab[POSE_PREV, n] = pose_prev
        tab[RGB_PREV, n] = rgb_prev
        tab[RGB_LAST, n] = rgb_last
        return carry

    lax.fori_loop(0, COUNT, chains, 0)

    def ends(p, carry):
        pose_end, rgb_end = COUNT, COUNT
        for m in range(COUNT):
            pose_end = jnp.where(tab[POSE_KEY, m] == p, m, pose_end)
            rgb_end = jnp.where(tab[RGB_KEY, m] == p, m, rgb_end)
        tab[POSE_END, p] = pose_end
        tab[RGB_END, p] = rgb_end
        return carry

    lax.fori_loop(0, NY * NZ, ends, 0)


def merge(ref, n, before, high, total, inner):
    old = ref[before, 0:1, :]
    top = jnp.maximum(old, high)
    keep = jnp.exp(old - top)
    add = jnp.exp(high - top)
    ref[n, 0:1, :] = top
    ref[n, 1:2, :] = ref[before, 1:2, :] * keep + total * add
    ref[n, 2:3, :] = ref[before, 2:3, :] * keep + inner * add


def slot_stats(n, tab, factor, qg, pose):
    pi, ri = tab[POSE, n], tab[RGB, n]
    q = qg[ri, 0]
    g = qg[ri, 1]
    both = pose[pi].reshape(2 * TILE, HD)
    pf = pose[pi, 0]
    dots = dot_t(q, both)
    score = dots[:, :TILE] * factor
    high = jnp.max(score, axis=0, keepdims=True)
    w = jnp.exp(score - high)
    pose_new = (
        high,
        jnp.sum(w, axis=0, keepdims=True),
        jnp.sum(w * dots[:, TILE:], axis=0, keepdims=True),
    )
    dots = dot_t(pf, qg[ri].reshape(2 * TILE, HD))
    score = dots[:, :TILE] * factor
    high = jnp.max(score, axis=0, keepdims=True)
    w = jnp.exp(score - high)
    rgb_new = (
        high,
        jnp.sum(w, axis=0, keepdims=True),
        jnp.sum(w * dots[:, TILE:], axis=0, keepdims=True),
    )
    return pose_new, rgb_new


TURNED = (((0,), (0,)), ((), ()))


def slot_before(n, tab, factor, qg, pose, rs):
    pi, ri = tab[POSE, n], tab[RGB, n]
    last = tab[RGB_LAST, n]
    inverse = 1.0 / jnp.maximum(rs[last, 1:2, :], 1.0)
    rows = jnp.concatenate(
        [rs[last, 0:1, :], inverse, rs[last, 2:3, :] * inverse, jnp.zeros((5, HD), jnp.float32)],
        axis=0,
    )
    rows = jnp.transpose(rows)
    q = qg[ri, 0]
    g = qg[ri, 1]
    both = pose[pi].reshape(2 * TILE, HD)
    dots = dot_t(q, both)
    score = dots[:, :TILE] * factor
    grad = dot_t(g, pose[pi, 0])
    pr = jnp.exp(score - rows[:, 0:1]) * rows[:, 1:2]
    own = pr * (grad - rows[:, 2:3])
    part = lax.dot_general(
        pr.astype(jnp.bfloat16), g, TURNED, preferred_element_type=jnp.float32
    )
    return score, own, dots[:, TILE:], part


def slot_after(n, tab, factor, qg, pose, fin, keep):
    pi, ri = tab[POSE, n], tab[RGB, n]
    zz, yy = pi // NY, pi % NY
    score = keep[0, n]
    pp = jnp.exp(score - fin[zz, pl.ds(yy, 1), :]) * fin[zz, pl.ds(4 + yy, 1), :]
    ds = keep[1, n] + pp * (keep[2, n] - fin[zz, pl.ds(8 + yy, 1), :])
    scale_part = jnp.sum((ds * score).reshape(TILE // 8, 8, HD), axis=0)
    scale_part = jnp.where(tab[POSE_KEY, n] >= 0, scale_part, 0.0)
    ds_low = (ds * factor).astype(jnp.bfloat16)
    pair = jnp.concatenate([ds_low, pp.astype(jnp.bfloat16)], axis=1)
    rgb_part = jnp.dot(
        pair, pose[pi].reshape(2 * TILE, HD), preferred_element_type=jnp.float32
    )
    pose_part = lax.dot_general(ds_low, qg[ri, 0], TURNED, preferred_element_type=jnp.float32)
    return rgb_part, pose_part, scale_part


def fused_kernel(
    rgb_ref, cot_ref, pf_ref, pc_ref, pairs_ref, scale,
    rgb_grad, pose_grad, scale_out, pairs_x,
    qg, pose, st, rs, keep, ex, got, fin, racc, pacc, sacc,
    rgbs, rbuf, sbuf, fbuf, land, sc, s_z, s_y, s_t, codes, tab,
    own_sem, codes_sem, y_send, y_recv, z_send, z_recv, b_send, b_recv,
    e1_send, e1_recv, e2_send, e2_recv,
    o_own, o_send, o_recv, r_send, r_recv, l_send, l_recv,
    sz_send, sz_recv, sy_send, sy_recv, st_send, st_recv,
):
    y, z = place()
    t = lax.axis_index("tm")
    sent = []

    def start(copy):
        copy.start()
        sent.append(copy)

    def y_parts(k):
        to = (y + k) % NY
        pos = 3 - k
        parts = [(pairs_ref, pairs_x.at[pos])]
        for h in range(2):
            cols = columns(to, h)
            parts += [
                (pf_ref.at[:, cols], pose[h].at[z * NY + y, 0]),
                (pc_ref.at[:, cols], pose[h].at[z * NY + y, 1]),
                (rgb_ref.at[:, :, cols], qg[h].at[pl.ds(pos * 4, 4), 0]),
                (cot_ref.at[:, :, cols], qg[h].at[pl.ds(pos * 4, 4), 1]),
            ]
        return parts

    def own(i):
        src, dst = y_parts(0)[i]
        return pltpu.make_async_copy(src, dst, own_sem.at[i])

    def across(k, i):
        src, dst = y_parts(k)[i]
        return remote(src, dst, y_send.at[k - 1, i], y_recv.at[k - 1, i], (y + k) % NY, z)

    def hop(h, side, step, c):
        block = (z + NZ - step) % NZ if side == 0 else (z + step) % NZ
        to = (z + 1) % NZ if side == 0 else (z + NZ - 1) % NZ
        ref = pose[h].at[block * NY + (y + NY - c) % NY]
        return remote(
            ref, ref, z_send.at[h, side, step, c], z_recv.at[h, side, step, c], y, to
        )

    def last_used(side, c):
        return (c < 2) == (side == 0)

    def begin(h, side, i):
        src, dst = y_parts(0)[1 + 4 * h + i]
        to = (z + 1) % NZ if side == 0 else (z + NZ - 1) % NZ
        return remote(src, dst, b_send.at[h, side, i], b_recv.at[h, side, i], y, to)

    def ring(h, step, c):
        if step == 0:
            across(c, 1 + 4 * h).wait_recv()
            across(c, 2 + 4 * h).wait_recv()
        for side in range(2):
            if step == 1 and c == 0:
                begin(h, side, 0).wait_recv()
                begin(h, side, 1).wait_recv()
            elif step > 0:
                hop(h, side, step - 1, c).wait_recv()
            if step < 3 or last_used(side, c):
                start(hop(h, side, step, c))

    def ring_all(h, step):
        for c in CHUNKS:
            ring(h, step, c)

    def ring_end(h):
        for c in range(NY):
            for side in range(2):
                if last_used(side, c):
                    hop(h, side, 3, c).wait_recv()

    def rgb_arrived(h):
        own(1 + 4 * h).wait()
        own(2 + 4 * h).wait()
        for i in (3 + 4 * h, 4 + 4 * h):
            for k in (1, 2, 3):
                across(k, i).wait_recv()
            own(i).wait()

    factor = [scale[2 * y + h] / math.sqrt(HD) for h in range(2)]

    def stats(h, low, high):
        def body(m, carry):
            slots = [STATS_UNROLL * m + u for u in range(STATS_UNROLL)]
            news = [slot_stats(n, tab, factor[h], qg[h], pose[h]) for n in slots]
            for n, (pose_new, rgb_new) in zip(slots, news):
                merge(st[h], n, tab[POSE_PREV, n], *pose_new)
                merge(rs[h], n, tab[RGB_PREV, n], *rgb_new)
            return carry

        lax.fori_loop(low, high, body, 0)

    def before(h, low, high):
        def body(m, carry):
            slots = [UNROLL * m + u for u in range(UNROLL)]
            news = [slot_before(n, tab, factor[h], qg[h], pose[h], rs[h]) for n in slots]
            for n, new in zip(slots, news):
                for i in range(3):
                    keep[i, n] = new[i]
                pacc[h][n] = new[3]
            return carry

        lax.fori_loop(low, high, body, 0)

    def after(h, low, high):
        def body(m, carry):
            slots = [UNROLL * m + u for u in range(UNROLL)]
            news = [slot_after(n, tab, factor[h], qg[h], pose[h], fin[h], keep) for n in slots]
            for n, new in zip(slots, news):
                racc[h][n] = racc[h][tab[RGB_PREV, n]] + new[0]
                pacc[h][n] = pacc[h][tab[POSE_PREV, n]] + (pacc[h][n] + new[1])
            sacc[h] += sum(new[2] for new in news)
            return carry

        lax.fori_loop(low, high, body, 0)

    def ex_copy(h, k):
        to = (z + k) % NZ
        return remote(
            ex[h].at[to], got[h].at[z], e1_send.at[h, k - 1], e1_recv.at[h, k - 1], y, to
        )

    def fin_copy(h, k):
        ref = fin[h].at[z]
        return remote(ref, ref, e2_send.at[h, k - 1], e2_recv.at[h, k - 1], y, (z + k) % NZ)

    def ex_first(h):
        def pack(zz, carry):
            for yy in range(NY):
                last = tab[POSE_END, zz * NY + yy]
                for i in range(3):
                    ex[h][zz, 4 * i + yy:4 * i + yy + 1, :] = st[h][last, i:i + 1, :]
            return carry

        lax.fori_loop(0, NZ, pack, 0)
        for k in range(1, NZ):
            start(ex_copy(h, k))
        got[h][z] = ex[h][z]

    def ex_second(h):
        for k in range(1, NZ):
            ex_copy(h, k).wait_recv()
        top = got[h][0, 0:4, :]
        for k in range(1, NZ):
            top = jnp.maximum(top, got[h][k, 0:4, :])
        total = jnp.zeros_like(top)
        inner = jnp.zeros_like(top)
        for k in range(NZ):
            keep = jnp.exp(got[h][k, 0:4, :] - top)
            total += got[h][k, 4:8, :] * keep
            inner += got[h][k, 8:12, :] * keep
        inverse = 1.0 / jnp.maximum(total, 1.0)
        fin[h][z, 0:4, :] = top
        fin[h][z, 4:8, :] = inverse
        fin[h][z, 8:12, :] = inner * inverse
        for k in range(1, NZ):
            start(fin_copy(h, k))

    def ex_end(h):
        for k in range(1, NZ):
            fin_copy(h, k).wait_recv()

    def rgb_copy(h, pos):
        src = rgbs[h].at[pos]
        dst = rgb_grad.at[:, :, columns(y, h)]
        if pos == 3:
            return pltpu.make_async_copy(src, dst, o_own.at[h])
        return remote(src, dst, o_send.at[h, pos], o_recv.at[h, pos], (y + 1 + pos) % NY, z)

    def rgb_send(h, pos):
        for i in range(4):
            rgbs[h][pos, i] = racc[h][tab[RGB_END, pos * 4 + i]].astype(jnp.bfloat16)
        rgb_copy(h, pos).start()

    def goal(side, step):
        return (z + 4 - step) % NZ if side == 0 else (z + 4 + step) % NZ

    def back(h, side, step, c):
        to = (z + 1) % NZ if side == 0 else (z + NZ - 1) % NZ
        if step == 3:
            return remote(
                sbuf[h].at[side, step, c], land[h].at[side, c],
                l_send.at[h, side, c], l_recv.at[h, side, c], (y + c) % NY, to,
            )
        return remote(
            sbuf[h].at[side, step, c], rbuf[h].at[side, step, c],
            r_send.at[h, side, step, c], r_recv.at[h, side, step, c], y, to,
        )

    def straight(h, c):
        return remote(
            fbuf[h].at[c], land[h].at[2, c], l_send.at[h, 2, c], l_recv.at[h, 2, c],
            (y + c) % NY, z,
        )

    def mine(h, block, c):
        return pacc[h][tab[POSE_END, block * NY + (y + c) % NY]]

    def back_one(h, side, step, c):
        value = mine(h, goal(side, step), c)
        if step > 1 or (step == 1 and last_used(side, c)):
            back(h, side, step - 1, c).wait_recv()
            value = value + rbuf[h][side, step - 1, c].astype(jnp.float32)
        sbuf[h][side, step, c] = value.astype(jnp.bfloat16)
        start(back(h, side, step, c))

    def back_step(h, phase):
        for late in range(2):
            step = phase + late
            if step > 3:
                continue
            for i in range(2):
                for side in range(2):
                    c = i + 2 * ((side + late) % 2)
                    back_one(h, side, step, c)
        if phase == 0:
            for c in range(1, NY):
                fbuf[h][c] = mine(h, z, c).astype(jnp.bfloat16)
                start(straight(h, c))

    def back_end(h):
        for c in (2, 3, 1, 0):
            if c == 0:
                value = mine(h, z, c)
            else:
                straight(h, c).wait_recv()
                value = land[h][2, c].astype(jnp.float32)
            for side in range(2):
                back(h, side, 3, c).wait_recv()
                value = value + land[h][side, c].astype(jnp.float32)
            pose_grad[:, columns((y + NY - c) % NY, h)] = value.astype(jnp.bfloat16)

    def z_scale(k):
        return remote(sc, s_z.at[z], sz_send.at[k - 1], sz_recv.at[k - 1], y, (z + k) % NZ)

    def y_scale(k):
        ref = s_y.at[y]
        return remote(ref, ref, sy_send.at[k - 1], sy_recv.at[k - 1], (y + k) % NY, z)

    def t_scale(k):
        ref = s_t.at[t]
        return remote_tm(ref, ref, st_send.at[k - 1], st_recv.at[k - 1], (t + k) % NT)

    def total_of(ref, count):
        total = ref[0]
        for k in range(1, count):
            total = total + ref[k]
        return total

    def scale_first():
        lane = lax.broadcasted_iota(jnp.int32, (8, HD), 1)
        tile = jnp.zeros((8, HD), jnp.float32)
        for h in range(2):
            part = jnp.sum(sacc[h], axis=0, keepdims=True)
            part = jnp.sum(part, axis=1, keepdims=True) / scale[2 * y + h]
            tile = jnp.where(lane == 2 * y + h, part, tile)
        sc[...] = tile
        for k in range(1, NZ):
            start(z_scale(k))
        s_z[z] = tile

    def scale_second():
        for k in range(1, NZ):
            z_scale(k).wait_recv()
        s_y[y] = total_of(s_z, NZ)
        for k in range(1, NY):
            start(y_scale(k))

    def scale_third():
        for k in range(1, NY):
            y_scale(k).wait_recv()
        s_t[t] = total_of(s_y, NY)
        for k in range(1, NT):
            start(t_scale(k))

    def scale_end():
        for k in range(1, NT):
            t_scale(k).wait_recv()
        scale_out[...] = total_of(s_t, NT)

    greet(
        [((y + k) % NY, z) for k in range(1, NY)]
        + [(y, (z + k) % NZ) for k in range(1, NZ)]
        + [((y + k) % NY, (z + side) % NZ) for k in range(1, NY) for side in (1, NZ - 1)],
        [(t + k) % NT for k in range(1, NT)],
    )
    for h in range(2):
        for i in range(2):
            for side in range(2):
                start(begin(h, side, i))
        for i in (1 + 4 * h, 2 + 4 * h):
            for k in (1, 2, 3):
                start(across(k, i))
    for k in (1, 2, 3):
        start(across(k, 0))
    for i in (0, 1, 2, 5, 6):
        own(i).start()
    for h in range(2):
        st[h][COUNT, 0:1, :] = jnp.full((1, HD), NEG, jnp.float32)
        rs[h][COUNT, 0:1, :] = jnp.full((1, HD), NEG, jnp.float32)
        st[h][COUNT, 1:3, :] = jnp.zeros((2, HD), jnp.float32)
        rs[h][COUNT, 1:3, :] = jnp.zeros((2, HD), jnp.float32)
        racc[h][COUNT] = jnp.zeros((TILE, HD), jnp.float32)
        pacc[h][COUNT] = jnp.zeros((TILE, HD), jnp.float32)
        sacc[h] = jnp.zeros((8, HD), jnp.float32)
    for c in CHUNKS[1:]:
        ring(0, 0, c)
    for i in (3, 4):
        for k in (1, 2, 3):
            start(across(k, i))
        own(i).start()
    for k in (1, 2, 3):
        across(k, 0).wait_recv()
    own(0).wait()
    to_codes = pltpu.make_async_copy(pairs_x, codes, codes_sem.at[0])
    to_codes.start()
    to_codes.wait()
    ring_all(0, 1)
    fill_table(codes, tab)
    ring_all(0, 2)
    ring_all(0, 3)
    for c in CHUNKS[1:]:
        ring(1, 0, c)
    for i in (7, 8):
        for k in (1, 2, 3):
            start(across(k, i))
        own(i).start()
    ring_end(0)
    rgb_arrived(0)
    ring(1, 1, CHUNKS[0])
    stats(0, 0, 1)
    ring(1, 1, CHUNKS[1])
    stats(0, 1, 2)
    ring(1, 1, CHUNKS[2])
    ex_first(0)
    ring(1, 1, CHUNKS[3])
    before(0, 0, 1)
    ring(1, 2, CHUNKS[0])
    before(0, 1, 2)
    ring(1, 2, CHUNKS[1])
    before(0, 2, 3)
    ring(1, 2, CHUNKS[2])
    ex_second(0)
    ring(1, 2, CHUNKS[3])
    before(0, 3, 4)
    for c in CHUNKS:
        ring(1, 3, c)
    ex_end(0)
    after(0, 0, 4)
    back_step(0, 0)
    for pos in range(4):
        rgb_send(0, pos)
    ring_end(1)
    rgb_arrived(1)
    stats(1, 0, 2)
    ex_first(1)
    back_step(0, 1)
    before(1, 0, 2)
    back_step(0, 2)
    ex_second(1)
    before(1, 2, 4)
    back_step(0, 3)
    ex_end(1)
    after(1, 0, 4)
    back_step(1, 0)
    scale_first()
    for pos in range(4):
        rgb_send(1, pos)
    back_step(1, 1)
    scale_second()
    back_end(0)
    back_step(1, 2)
    scale_third()
    back_step(1, 3)
    back_end(1)
    scale_end()
    for h in range(2):
        for pos in range(4):
            rgb_copy(h, pos).wait()
    for copy in sent:
        copy.wait_send()


def fused(rgb, cot, pf, pc, pairs, scale):
    dma = pltpu.SemaphoreType.DMA
    low, full = jnp.bfloat16, jnp.float32

    def twice(shape, kind):
        return [pltpu.VMEM(shape, kind)] * 2

    return pl.pallas_call(
        fused_kernel,
        out_shape=(
            jax.ShapeDtypeStruct((4, TILE, 1024), low),
            jax.ShapeDtypeStruct((TILE, 1024), low),
            jax.ShapeDtypeStruct((8, HD), full),
            jax.ShapeDtypeStruct((NY, 1, SLOTS), jnp.int32),
        ),
        in_specs=[HBM] * 5 + [SM],
        out_specs=(VM, VM, VM, HBM),
        scratch_shapes=[
            twice((16, 2, TILE, HD), low),
            twice((NY * NZ, 2, TILE, HD), low),
            twice((COUNT + 1, 8, HD), full),
            twice((COUNT + 1, 8, HD), full),
            pltpu.VMEM((3, COUNT, TILE, HD), full),
            twice((NZ, 16, HD), full),
            twice((NZ, 16, HD), full),
            twice((NZ, 16, HD), full),
            twice((COUNT + 1, TILE, HD), full),
            twice((COUNT + 1, TILE, HD), full),
            pltpu.VMEM((2, 8, HD), full),
            twice((4, 4, TILE, HD), low),
            twice((2, 3, NY, TILE, HD), low),
            twice((2, 4, NY, TILE, HD), low),
            twice((NY, TILE, HD), low),
            twice((3, NY, TILE, HD), low),
            pltpu.VMEM((8, HD), full),
            pltpu.VMEM((NZ, 8, HD), full),
            pltpu.VMEM((NY, 8, HD), full),
            pltpu.VMEM((NT, 8, HD), full),
            pltpu.SMEM((NY, 1, SLOTS), jnp.int32),
            pltpu.SMEM((9, NY * NZ), jnp.int32),
            dma((9,)), dma((1,)), dma((3, 9)), dma((3, 9)),
            dma((2, 2, 4, NY)), dma((2, 2, 4, NY)), dma((2, 2, 2)), dma((2, 2, 2)),
            dma((2, NZ - 1)), dma((2, NZ - 1)), dma((2, NZ - 1)), dma((2, NZ - 1)),
            dma((2,)), dma((2, 3)), dma((2, 3)),
            dma((2, 2, 3, NY)), dma((2, 2, 3, NY)),
            dma((2, 3, NY)), dma((2, 3, NY)),
            dma((NZ - 1,)), dma((NZ - 1,)),
            dma((NY - 1,)), dma((NY - 1,)),
            dma((NT - 1,)), dma((NT - 1,)),
        ],
        compiler_params=pltpu.CompilerParams(
            collective_id=0, has_side_effects=True, vmem_limit_bytes=VMEM_LIMIT
        ),
    )(rgb, cot, pf, pc, pairs, scale)


def finish_kernel(rgb, pose, scale, rgb_out, pose_out, scale_out, sem):
    copies = [
        pltpu.make_async_copy(rgb.at[i], rgb_out.at[i], sem.at[i]) for i in range(4)
    ] + [pltpu.make_async_copy(pose, pose_out, sem.at[4])]
    for copy in copies:
        copy.start()
    scale_out[...] = scale[0:1, 0:8]
    for copy in copies:
        copy.wait()


def finish(rgb, pose, scale):
    return pl.pallas_call(
        finish_kernel,
        out_shape=(
            jax.ShapeDtypeStruct(rgb.shape, rgb.dtype),
            jax.ShapeDtypeStruct(pose.shape, pose.dtype),
            jax.ShapeDtypeStruct((1, 8), jnp.float32),
        ),
        in_specs=[VM, VM, VM],
        out_specs=(HBM, HBM, VM),
        scratch_shapes=[pltpu.SemaphoreType.DMA((5,))],
        compiler_params=pltpu.CompilerParams(vmem_limit_bytes=VMEM_LIMIT),
    )(rgb, pose, scale)


def local(rgb_feat, rgb_grad_out, pose_feat, pose_grad_out, logit_scale, pairs):
    rgb_grad, pose_grad, scale_grad, _ = fused(
        *(
            pltpu.with_memory_space_constraint(part, pltpu.HBM)
            for part in (
                rgb_feat.reshape(4, TILE, 1024),
                rgb_grad_out.reshape(4, TILE, 1024),
                pose_feat[0],
                pose_grad_out[0],
                pairs,
            )
        ),
        pltpu.with_memory_space_constraint(logit_scale, pltpu.HBM),
    )
    rgb_grad, pose_grad, scale_grad = finish(rgb_grad, pose_grad, scale_grad)
    return rgb_grad.reshape(1, 512, 1024), pose_grad[None], scale_grad[0]


def solution(mesh):
    return jax.shard_map(
        local,
        mesh=mesh,
        in_specs=(
            P("tm", "seq", None),
            P("tm", "seq", None),
            P("tm", "seq", None),
            P("tm", "seq", None),
            P(),
            P("tm", "seq"),
        ),
        out_specs=(P("tm", "seq", None), P("tm", "seq", None), P()),
        check_vma=False,
    )
```

```python
import math

import jax
import jax.numpy as jnp
from jax import lax
from jax.experimental import pallas as pl
from jax.experimental.pallas import tpu as pltpu
from jax.sharding import PartitionSpec as P

NEG = -1e30
NY = 4
NZ = 8
NT = 8
TILE = 128
HD = 128
SLOTS = 5
COUNT = NY * SLOTS
VMEM_LIMIT = 28 * 1024 * 1024
MESH = pl.DeviceIdType.MESH
ANY = pl.BlockSpec(memory_space=pl.ANY)
HBM = pl.BlockSpec(memory_space=pltpu.HBM)
VM = pl.BlockSpec(memory_space=pltpu.VMEM)
SM = pl.BlockSpec(memory_space=pltpu.SMEM)
POSE, RGB, POSE_KEY, RGB_KEY, POSE_PREV, RGB_PREV, RGB_LAST, POSE_END, RGB_END = range(9)
CHUNKS = (0, 1, 3, 2)
FAR = (4, 3, 5, 2, 6, 1, 7)
STATS_UNROLL = 10
UNROLL = 5


def place():
    me = lax.axis_index("seq")
    return me // NZ, me % NZ


def remote(src, dst, send_sem, recv_sem, y, z):
    return pltpu.make_async_remote_copy(
        src_ref=src,
        dst_ref=dst,
        send_sem=send_sem,
        recv_sem=recv_sem,
        device_id={"seq": y * NZ + z},
        device_id_type=MESH,
    )


def remote_tm(src, dst, send_sem, recv_sem, t):
    return pltpu.make_async_remote_copy(
        src_ref=src,
        dst_ref=dst,
        send_sem=send_sem,
        recv_sem=recv_sem,
        device_id={"tm": t},
        device_id_type=MESH,
    )


def greet(seqs, tms=()):
    barrier = pltpu.get_barrier_semaphore()
    for y, z in seqs:
        pl.semaphore_signal(
            barrier, inc=1, device_id={"seq": y * NZ + z}, device_id_type=MESH
        )
    for t in tms:
        pl.semaphore_signal(barrier, inc=1, device_id={"tm": t}, device_id_type=MESH)
    pl.semaphore_wait(barrier, len(seqs) + len(tms))


def columns(y, h):
    return pl.ds(pl.multiple_of((2 * y + h) * HD, HD), HD)


def dot_t(a, b):
    return lax.dot_general(a, b, (((1,), (1,)), ((), ())), preferred_element_type=jnp.float32)


def fill_table(codes, tab):
    def slots(n, carry):
        pos = (n // 10) * 2 + n % 2
        code = codes[pos, 0, (n % 10) // 2]
        kept = jnp.maximum(code, 0)
        tile = kept % (NY * NZ)
        pi = (tile % NZ) * NY + tile // NZ
        ri = pos * 4 + kept // (NY * NZ)
        tab[POSE, n] = pi
        tab[RGB, n] = ri
        tab[POSE_KEY, n] = jnp.where(code >= 0, pi, -1 - n)
        tab[RGB_KEY, n] = jnp.where(code >= 0, ri, -1 - n)
        return carry

    lax.fori_loop(0, COUNT, slots, 0)

    def chains(n, carry):
        pose_key, rgb_key = tab[POSE_KEY, n], tab[RGB_KEY, n]
        pose_prev, rgb_prev, rgb_last = COUNT, COUNT, COUNT
        for m in range(COUNT):
            same_rgb = tab[RGB_KEY, m] == rgb_key
            early = n > m
            pose_prev = jnp.where((tab[POSE_KEY, m] == pose_key) & early, m, pose_prev)
            rgb_prev = jnp.where(same_rgb & early, m, rgb_prev)
            rgb_last = jnp.where(same_rgb, m, rgb_last)
        tab[POSE_PREV, n] = pose_prev
        tab[RGB_PREV, n] = rgb_prev
        tab[RGB_LAST, n] = rgb_last
        return carry

    lax.fori_loop(0, COUNT, chains, 0)

    def ends(p, carry):
        pose_end, rgb_end = COUNT, COUNT
        for m in range(COUNT):
            pose_end = jnp.where(tab[POSE_KEY, m] == p, m, pose_end)
            rgb_end = jnp.where(tab[RGB_KEY, m] == p, m, rgb_end)
        tab[POSE_END, p] = pose_end
        tab[RGB_END, p] = rgb_end
        return carry

    lax.fori_loop(0, NY * NZ, ends, 0)


def merge(ref, n, before, high, total, inner):
    old = ref[before, 0:1, :]
    top = jnp.maximum(old, high)
    keep = jnp.exp(old - top)
    add = jnp.exp(high - top)
    ref[n, 0:1, :] = top
    ref[n, 1:2, :] = ref[before, 1:2, :] * keep + total * add
    ref[n, 2:3, :] = ref[before, 2:3, :] * keep + inner * add


def slot_stats(n, tab, factor, qg, pose):
    pi, ri = tab[POSE, n], tab[RGB, n]
    q = qg[ri, 0]
    g = qg[ri, 1]
    both = pose[pi].reshape(2 * TILE, HD)
    pf = pose[pi, 0]
    dots = dot_t(q, both)
    score = dots[:, :TILE] * factor
    high = jnp.max(score, axis=0, keepdims=True)
    w = jnp.exp(score - high)
    pose_new = (
        high,
        jnp.sum(w, axis=0, keepdims=True),
        jnp.sum(w * dots[:, TILE:], axis=0, keepdims=True),
    )
    dots = dot_t(pf, qg[ri].reshape(2 * TILE, HD))
    score = dots[:, :TILE] * factor
    high = jnp.max(score, axis=0, keepdims=True)
    w = jnp.exp(score - high)
    rgb_new = (
        high,
        jnp.sum(w, axis=0, keepdims=True),
        jnp.sum(w * dots[:, TILE:], axis=0, keepdims=True),
    )
    return pose_new, rgb_new


TURNED = (((0,), (0,)), ((), ()))


def slot_before(n, tab, factor, qg, pose, rs):
    pi, ri = tab[POSE, n], tab[RGB, n]
    last = tab[RGB_LAST, n]
    inverse = 1.0 / jnp.maximum(rs[last, 1:2, :], 1.0)
    rows = jnp.concatenate(
        [rs[last, 0:1, :], inverse, rs[last, 2:3, :] * inverse, jnp.zeros((5, HD), jnp.float32)],
        axis=0,
    )
    rows = jnp.transpose(rows)
    q = qg[ri, 0]
    g = qg[ri, 1]
    both = pose[pi].reshape(2 * TILE, HD)
    dots = dot_t(q, both)
    score = dots[:, :TILE] * factor
    grad = dot_t(g, pose[pi, 0])
    pr = jnp.exp(score - rows[:, 0:1]) * rows[:, 1:2]
    own = pr * (grad - rows[:, 2:3])
    part = lax.dot_general(
        pr.astype(jnp.bfloat16), g, TURNED, preferred_element_type=jnp.float32
    )
    return score, own, dots[:, TILE:], part


def slot_after(n, tab, factor, qg, pose, fin, keep):
    pi, ri = tab[POSE, n], tab[RGB, n]
    zz, yy = pi // NY, pi % NY
    score = keep[0, n]
    pp = jnp.exp(score - fin[zz, pl.ds(yy, 1), :]) * fin[zz, pl.ds(4 + yy, 1), :]
    ds = keep[1, n] + pp * (keep[2, n] - fin[zz, pl.ds(8 + yy, 1), :])
    scale_part = jnp.sum((ds * score).reshape(TILE // 8, 8, HD), axis=0)
    scale_part = jnp.where(tab[POSE_KEY, n] >= 0, scale_part, 0.0)
    ds_low = (ds * factor).astype(jnp.bfloat16)
    pair = jnp.concatenate([ds_low, pp.astype(jnp.bfloat16)], axis=1)
    rgb_part = jnp.dot(
        pair, pose[pi].reshape(2 * TILE, HD), preferred_element_type=jnp.float32
    )
    pose_part = lax.dot_general(ds_low, qg[ri, 0], TURNED, preferred_element_type=jnp.float32)
    return rgb_part, pose_part, scale_part


def fused_kernel(
    rgb_ref, cot_ref, pf_ref, pc_ref, pairs_ref, scale,
    rgb_grad, pose_grad, scale_out, pairs_x,
    qg, pose, st, rs, keep, ex, got, fin, racc, pacc, sacc,
    rgbs, rbuf, sbuf, fbuf, land, sc, s_z, s_y, s_t, codes, tab,
    own_sem, codes_sem, y_send, y_recv, z_send, z_recv, b_send, b_recv,
    e1_send, e1_recv, e2_send, e2_recv,
    o_own, o_send, o_recv, r_send, r_recv, l_send, l_recv,
    sz_send, sz_recv, sy_send, sy_recv, st_send, st_recv,
):
    y, z = place()
    t = lax.axis_index("tm")
    sent = []

    def start(copy):
        copy.start()
        sent.append(copy)

    def y_parts(k):
        to = (y + k) % NY
        pos = 3 - k
        parts = [(pairs_ref, pairs_x.at[pos])]
        for h in range(2):
            cols = columns(to, h)
            parts += [
                (pf_ref.at[:, cols], pose[h].at[z * NY + y, 0]),
                (pc_ref.at[:, cols], pose[h].at[z * NY + y, 1]),
                (rgb_ref.at[:, :, cols], qg[h].at[pl.ds(pos * 4, 4), 0]),
                (cot_ref.at[:, :, cols], qg[h].at[pl.ds(pos * 4, 4), 1]),
            ]
        return parts

    def own(i):
        src, dst = y_parts(0)[i]
        return pltpu.make_async_copy(src, dst, own_sem.at[i])

    def across(k, i):
        src, dst = y_parts(k)[i]
        return remote(src, dst, y_send.at[k - 1, i], y_recv.at[k - 1, i], (y + k) % NY, z)

    def hop(h, side, step, c):
        block = (z + NZ - step) % NZ if side == 0 else (z + step) % NZ
        to = (z + 1) % NZ if side == 0 else (z + NZ - 1) % NZ
        ref = pose[h].at[block * NY + (y + NY - c) % NY]
        return remote(
            ref, ref, z_send.at[h, side, step, c], z_recv.at[h, side, step, c], y, to
        )

    def last_used(side, c):
        return (c < 2) == (side == 0)

    def begin(h, side, i):
        src, dst = y_parts(0)[1 + 4 * h + i]
        to = (z + 1) % NZ if side == 0 else (z + NZ - 1) % NZ
        return remote(src, dst, b_send.at[h, side, i], b_recv.at[h, side, i], y, to)

    def ring(h, step, c):
        if step == 0:
            across(c, 1 + 4 * h).wait_recv()
            across(c, 2 + 4 * h).wait_recv()
        for side in range(2):
            if step == 1 and c == 0:
                begin(h, side, 0).wait_recv()
                begin(h, side, 1).wait_recv()
            elif step > 0:
                hop(h, side, step - 1, c).wait_recv()
            if step < 3 or last_used(side, c):
                start(hop(h, side, step, c))

    def ring_all(h, step):
        for c in CHUNKS:
            ring(h, step, c)

    def ring_end(h):
        for c in range(NY):
            for side in range(2):
                if last_used(side, c):
                    hop(h, side, 3, c).wait_recv()

    def rgb_arrived(h):
        own(1 + 4 * h).wait()
        own(2 + 4 * h).wait()
        for i in (3 + 4 * h, 4 + 4 * h):
            for k in (1, 2, 3):
                across(k, i).wait_recv()
            own(i).wait()

    factor = [scale[2 * y + h] / math.sqrt(HD) for h in range(2)]

    def stats(h, low, high):
        def body(m, carry):
            slots = [STATS_UNROLL * m + u for u in range(STATS_UNROLL)]
            news = [slot_stats(n, tab, factor[h], qg[h], pose[h]) for n in slots]
            for n, (pose_new, rgb_new) in zip(slots, news):
                merge(st[h], n, tab[POSE_PREV, n], *pose_new)
                merge(rs[h], n, tab[RGB_PREV, n], *rgb_new)
            return carry

        lax.fori_loop(low, high, body, 0)

    def before(h, low, high):
        def body(m, carry):
            slots = [UNROLL * m + u for u in range(UNROLL)]
            news = [slot_before(n, tab, factor[h], qg[h], pose[h], rs[h]) for n in slots]
            for n, new in zip(slots, news):
                for i in range(3):
                    keep[i, n] = new[i]
                pacc[h][n] = new[3]
            return carry

        lax.fori_loop(low, high, body, 0)

    def after(h, low, high):
        def body(m, carry):
            slots = [UNROLL * m + u for u in range(UNROLL)]
            news = [slot_after(n, tab, factor[h], qg[h], pose[h], fin[h], keep) for n in slots]
            for n, new in zip(slots, news):
                racc[h][n] = racc[h][tab[RGB_PREV, n]] + new[0]
                pacc[h][n] = pacc[h][tab[POSE_PREV, n]] + (pacc[h][n] + new[1])
            sacc[h] += sum(new[2] for new in news)
            return carry

        lax.fori_loop(low, high, body, 0)

    def ex_copy(h, k):
        to = (z + k) % NZ
        return remote(
            ex[h].at[to], got[h].at[z], e1_send.at[h, k - 1], e1_recv.at[h, k - 1], y, to
        )

    def fin_copy(h, k):
        ref = fin[h].at[z]
        return remote(ref, ref, e2_send.at[h, k - 1], e2_recv.at[h, k - 1], y, (z + k) % NZ)

    def ex_first(h):
        def pack(zz):
            for yy in range(NY):
                last = tab[POSE_END, zz * NY + yy]
                for i in range(3):
                    ex[h][zz, 4 * i + yy:4 * i + yy + 1, :] = st[h][last, i:i + 1, :]

        for k in FAR:
            pack((z + k) % NZ)
            start(ex_copy(h, k))
        pack(z)
        got[h][z] = ex[h][z]

    def ex_second(h):
        for k in range(1, NZ):
            ex_copy(h, k).wait_recv()
        top = got[h][0, 0:4, :]
        for k in range(1, NZ):
            top = jnp.maximum(top, got[h][k, 0:4, :])
        total = jnp.zeros_like(top)
        inner = jnp.zeros_like(top)
        for k in range(NZ):
            keep = jnp.exp(got[h][k, 0:4, :] - top)
            total += got[h][k, 4:8, :] * keep
            inner += got[h][k, 8:12, :] * keep
        inverse = 1.0 / jnp.maximum(total, 1.0)
        fin[h][z, 0:4, :] = top
        fin[h][z, 4:8, :] = inverse
        fin[h][z, 8:12, :] = inner * inverse
        for k in FAR:
            start(fin_copy(h, k))

    def ex_end(h):
        for k in range(1, NZ):
            fin_copy(h, k).wait_recv()

    def rgb_copy(h, pos):
        src = rgbs[h].at[pos]
        dst = rgb_grad.at[:, :, columns(y, h)]
        if pos == 3:
            return pltpu.make_async_copy(src, dst, o_own.at[h])
        return remote(src, dst, o_send.at[h, pos], o_recv.at[h, pos], (y + 1 + pos) % NY, z)

    def rgb_send(h, pos):
        for i in range(4):
            rgbs[h][pos, i] = racc[h][tab[RGB_END, pos * 4 + i]].astype(jnp.bfloat16)
        rgb_copy(h, pos).start()

    def goal(side, step):
        return (z + 4 - step) % NZ if side == 0 else (z + 4 + step) % NZ

    def back(h, side, step, c):
        to = (z + 1) % NZ if side == 0 else (z + NZ - 1) % NZ
        if step == 3:
            return remote(
                sbuf[h].at[side, step, c], land[h].at[side, c],
                l_send.at[h, side, c], l_recv.at[h, side, c], (y + c) % NY, to,
            )
        return remote(
            sbuf[h].at[side, step, c], rbuf[h].at[side, step, c],
            r_send.at[h, side, step, c], r_recv.at[h, side, step, c], y, to,
        )

    def straight(h, c):
        return remote(
            fbuf[h].at[c], land[h].at[2, c], l_send.at[h, 2, c], l_recv.at[h, 2, c],
            (y + c) % NY, z,
        )

    def mine(h, block, c):
        return pacc[h][tab[POSE_END, block * NY + (y + c) % NY]]

    def back_one(h, side, step, c):
        value = mine(h, goal(side, step), c)
        if step > 1 or (step == 1 and last_used(side, c)):
            back(h, side, step - 1, c).wait_recv()
            value = value + rbuf[h][side, step - 1, c].astype(jnp.float32)
        sbuf[h][side, step, c] = value.astype(jnp.bfloat16)
        start(back(h, side, step, c))

    def back_step(h, phase):
        for late in range(2):
            step = phase + late
            if step > 3:
                continue
            for i in range(2):
                for side in range(2):
                    c = i + 2 * ((side + late) % 2)
                    back_one(h, side, step, c)
        if phase == 0:
            for c in range(1, NY):
                fbuf[h][c] = mine(h, z, c).astype(jnp.bfloat16)
                start(straight(h, c))

    def back_end(h):
        for c in (2, 3, 1, 0):
            if c == 0:
                value = mine(h, z, c)
            else:
                straight(h, c).wait_recv()
                value = land[h][2, c].astype(jnp.float32)
            for side in range(2):
                back(h, side, 3, c).wait_recv()
                value = value + land[h][side, c].astype(jnp.float32)
            pose_grad[:, columns((y + NY - c) % NY, h)] = value.astype(jnp.bfloat16)

    def z_scale(k):
        return remote(sc, s_z.at[z], sz_send.at[k - 1], sz_recv.at[k - 1], y, (z + k) % NZ)

    def y_scale(k):
        ref = s_y.at[y]
        return remote(ref, ref, sy_send.at[k - 1], sy_recv.at[k - 1], (y + k) % NY, z)

    def t_scale(k):
        ref = s_t.at[t]
        return remote_tm(ref, ref, st_send.at[k - 1], st_recv.at[k - 1], (t + k) % NT)

    def total_of(ref, count):
        total = ref[0]
        for k in range(1, count):
            total = total + ref[k]
        return total

    def scale_first():
        lane = lax.broadcasted_iota(jnp.int32, (8, HD), 1)
        tile = jnp.zeros((8, HD), jnp.float32)
        for h in range(2):
            part = jnp.sum(sacc[h], axis=0, keepdims=True)
            part = jnp.sum(part, axis=1, keepdims=True) / scale[2 * y + h]
            tile = jnp.where(lane == 2 * y + h, part, tile)
        sc[...] = tile
        for k in FAR:
            start(z_scale(k))
        s_z[z] = tile

    def scale_second():
        for k in range(1, NZ):
            z_scale(k).wait_recv()
        s_y[y] = total_of(s_z, NZ)
        for k in range(1, NY):
            start(y_scale(k))

    def scale_third():
        for k in range(1, NY):
            y_scale(k).wait_recv()
        s_t[t] = total_of(s_y, NY)
        for k in range(1, NT):
            start(t_scale(k))

    def scale_end():
        for k in range(1, NT):
            t_scale(k).wait_recv()
        scale_out[...] = total_of(s_t, NT)

    greet(
        [((y + k) % NY, z) for k in range(1, NY)]
        + [(y, (z + k) % NZ) for k in range(1, NZ)]
        + [((y + k) % NY, (z + side) % NZ) for k in range(1, NY) for side in (1, NZ - 1)],
        [(t + k) % NT for k in range(1, NT)],
    )
    for h in range(2):
        for i in range(2):
            for side in range(2):
                start(begin(h, side, i))
        for i in (1 + 4 * h, 2 + 4 * h):
            for k in (1, 2, 3):
                start(across(k, i))
    for k in (1, 2, 3):
        start(across(k, 0))
    for i in (0, 1, 2, 5, 6):
        own(i).start()
    for h in range(2):
        st[h][COUNT, 0:1, :] = jnp.full((1, HD), NEG, jnp.float32)
        rs[h][COUNT, 0:1, :] = jnp.full((1, HD), NEG, jnp.float32)
        st[h][COUNT, 1:3, :] = jnp.zeros((2, HD), jnp.float32)
        rs[h][COUNT, 1:3, :] = jnp.zeros((2, HD), jnp.float32)
        racc[h][COUNT] = jnp.zeros((TILE, HD), jnp.float32)
        pacc[h][COUNT] = jnp.zeros((TILE, HD), jnp.float32)
        sacc[h] = jnp.zeros((8, HD), jnp.float32)
    for c in CHUNKS[1:]:
        ring(0, 0, c)
    for i in (3, 4):
        for k in (1, 2, 3):
            start(across(k, i))
        own(i).start()
    for k in (1, 2, 3):
        across(k, 0).wait_recv()
    own(0).wait()
    to_codes = pltpu.make_async_copy(pairs_x, codes, codes_sem.at[0])
    to_codes.start()
    to_codes.wait()
    ring_all(0, 1)
    fill_table(codes, tab)
    ring_all(0, 2)
    ring_all(0, 3)
    for c in CHUNKS[1:]:
        ring(1, 0, c)
    for i in (7, 8):
        for k in (1, 2, 3):
            start(across(k, i))
        own(i).start()
    ring_end(0)
    rgb_arrived(0)
    ring(1, 1, CHUNKS[0])
    stats(0, 0, 1)
    ring(1, 1, CHUNKS[1])
    stats(0, 1, 2)
    ring(1, 1, CHUNKS[2])
    ex_first(0)
    ring(1, 1, CHUNKS[3])
    before(0, 0, 1)
    ring(1, 2, CHUNKS[0])
    before(0, 1, 2)
    ring(1, 2, CHUNKS[1])
    before(0, 2, 3)
    ring(1, 2, CHUNKS[2])
    ex_second(0)
    ring(1, 2, CHUNKS[3])
    before(0, 3, 4)
    for c in CHUNKS:
        ring(1, 3, c)
    ex_end(0)
    after(0, 0, 4)
    back_step(0, 0)
    for pos in range(4):
        rgb_send(0, pos)
    ring_end(1)
    rgb_arrived(1)
    stats(1, 0, 2)
    ex_first(1)
    back_step(0, 1)
    before(1, 0, 2)
    back_step(0, 2)
    ex_second(1)
    before(1, 2, 4)
    back_step(0, 3)
    ex_end(1)
    after(1, 0, 4)
    back_step(1, 0)
    scale_first()
    for pos in range(4):
        rgb_send(1, pos)
    back_step(1, 1)
    scale_second()
    back_end(0)
    back_step(1, 2)
    scale_third()
    back_step(1, 3)
    back_end(1)
    scale_end()
    for h in range(2):
        for pos in range(4):
            rgb_copy(h, pos).wait()
    for copy in sent:
        copy.wait_send()


def fused(rgb, cot, pf, pc, pairs, scale):
    dma = pltpu.SemaphoreType.DMA
    low, full = jnp.bfloat16, jnp.float32

    def twice(shape, kind):
        return [pltpu.VMEM(shape, kind)] * 2

    return pl.pallas_call(
        fused_kernel,
        out_shape=(
            jax.ShapeDtypeStruct((4, TILE, 1024), low),
            jax.ShapeDtypeStruct((TILE, 1024), low),
            jax.ShapeDtypeStruct((8, HD), full),
            jax.ShapeDtypeStruct((NY, 1, SLOTS), jnp.int32),
        ),
        in_specs=[HBM] * 5 + [SM],
        out_specs=(VM, VM, VM, HBM),
        scratch_shapes=[
            twice((16, 2, TILE, HD), low),
            twice((NY * NZ, 2, TILE, HD), low),
            twice((COUNT + 1, 8, HD), full),
            twice((COUNT + 1, 8, HD), full),
            pltpu.VMEM((3, COUNT, TILE, HD), full),
            twice((NZ, 16, HD), full),
            twice((NZ, 16, HD), full),
            twice((NZ, 16, HD), full),
            twice((COUNT + 1, TILE, HD), full),
            twice((COUNT + 1, TILE, HD), full),
            pltpu.VMEM((2, 8, HD), full),
            twice((4, 4, TILE, HD), low),
            twice((2, 3, NY, TILE, HD), low),
            twice((2, 4, NY, TILE, HD), low),
            twice((NY, TILE, HD), low),
            twice((3, NY, TILE, HD), low),
            pltpu.VMEM((8, HD), full),
            pltpu.VMEM((NZ, 8, HD), full),
            pltpu.VMEM((NY, 8, HD), full),
            pltpu.VMEM((NT, 8, HD), full),
            pltpu.SMEM((NY, 1, SLOTS), jnp.int32),
            pltpu.SMEM((9, NY * NZ), jnp.int32),
            dma((9,)), dma((1,)), dma((3, 9)), dma((3, 9)),
            dma((2, 2, 4, NY)), dma((2, 2, 4, NY)), dma((2, 2, 2)), dma((2, 2, 2)),
            dma((2, NZ - 1)), dma((2, NZ - 1)), dma((2, NZ - 1)), dma((2, NZ - 1)),
            dma((2,)), dma((2, 3)), dma((2, 3)),
            dma((2, 2, 3, NY)), dma((2, 2, 3, NY)),
            dma((2, 3, NY)), dma((2, 3, NY)),
            dma((NZ - 1,)), dma((NZ - 1,)),
            dma((NY - 1,)), dma((NY - 1,)),
            dma((NT - 1,)), dma((NT - 1,)),
        ],
        compiler_params=pltpu.CompilerParams(
            collective_id=0, has_side_effects=True, vmem_limit_bytes=VMEM_LIMIT
        ),
    )(rgb, cot, pf, pc, pairs, scale)


def finish_kernel(rgb, pose, scale, rgb_out, pose_out, scale_out, sem):
    copies = [
        pltpu.make_async_copy(rgb.at[i], rgb_out.at[i], sem.at[i]) for i in range(4)
    ] + [pltpu.make_async_copy(pose, pose_out, sem.at[4])]
    for copy in copies:
        copy.start()
    scale_out[...] = scale[0:1, 0:8]
    for copy in copies:
        copy.wait()


def finish(rgb, pose, scale):
    return pl.pallas_call(
        finish_kernel,
        out_shape=(
            jax.ShapeDtypeStruct(rgb.shape, rgb.dtype),
            jax.ShapeDtypeStruct(pose.shape, pose.dtype),
            jax.ShapeDtypeStruct((1, 8), jnp.float32),
        ),
        in_specs=[VM, VM, VM],
        out_specs=(HBM, HBM, VM),
        scratch_shapes=[pltpu.SemaphoreType.DMA((5,))],
        compiler_params=pltpu.CompilerParams(vmem_limit_bytes=VMEM_LIMIT),
    )(rgb, pose, scale)


def local(rgb_feat, rgb_grad_out, pose_feat, pose_grad_out, logit_scale, pairs):
    rgb_grad, pose_grad, scale_grad, _ = fused(
        *(
            pltpu.with_memory_space_constraint(part, pltpu.HBM)
            for part in (
                rgb_feat.reshape(4, TILE, 1024),
                rgb_grad_out.reshape(4, TILE, 1024),
                pose_feat[0],
                pose_grad_out[0],
                pairs,
            )
        ),
        pltpu.with_memory_space_constraint(logit_scale, pltpu.HBM),
    )
    rgb_grad, pose_grad, scale_grad = finish(rgb_grad, pose_grad, scale_grad)
    return rgb_grad.reshape(1, 512, 1024), pose_grad[None], scale_grad[0]


def solution(mesh):
    return jax.shard_map(
        local,
        mesh=mesh,
        in_specs=(
            P("tm", "seq", None),
            P("tm", "seq", None),
            P("tm", "seq", None),
            P("tm", "seq", None),
            P(),
            P("tm", "seq"),
        ),
        out_specs=(P("tm", "seq", None), P("tm", "seq", None), P()),
        check_vma=False,
    )
```

```python
import math

import jax
import jax.numpy as jnp
from jax import lax
from jax.experimental import pallas as pl
from jax.experimental.pallas import tpu as pltpu
from jax.sharding import PartitionSpec as P

NEG = -1e30
NY = 4
NZ = 8
NT = 8
TILE = 128
HD = 128
SLOTS = 5
COUNT = NY * SLOTS
VMEM_LIMIT = 28 * 1024 * 1024
MESH = pl.DeviceIdType.MESH
ANY = pl.BlockSpec(memory_space=pl.ANY)
HBM = pl.BlockSpec(memory_space=pltpu.HBM)
VM = pl.BlockSpec(memory_space=pltpu.VMEM)
SM = pl.BlockSpec(memory_space=pltpu.SMEM)
POSE, RGB, POSE_KEY, RGB_KEY, POSE_PREV, RGB_PREV, RGB_LAST, POSE_END, RGB_END = range(9)
CHUNKS = (0, 1, 3, 2)
FAR = (4, 3, 5, 2, 6, 1, 7)
ACROSS = (2, 1, 3)
STATS_UNROLL = 10
UNROLL = 5


def place():
    me = lax.axis_index("seq")
    return me // NZ, me % NZ


def remote(src, dst, send_sem, recv_sem, y, z):
    return pltpu.make_async_remote_copy(
        src_ref=src,
        dst_ref=dst,
        send_sem=send_sem,
        recv_sem=recv_sem,
        device_id={"seq": y * NZ + z},
        device_id_type=MESH,
    )


def remote_tm(src, dst, send_sem, recv_sem, t):
    return pltpu.make_async_remote_copy(
        src_ref=src,
        dst_ref=dst,
        send_sem=send_sem,
        recv_sem=recv_sem,
        device_id={"tm": t},
        device_id_type=MESH,
    )


def greet(seqs, tms=()):
    barrier = pltpu.get_barrier_semaphore()
    for y, z in seqs:
        pl.semaphore_signal(
            barrier, inc=1, device_id={"seq": y * NZ + z}, device_id_type=MESH
        )
    for t in tms:
        pl.semaphore_signal(barrier, inc=1, device_id={"tm": t}, device_id_type=MESH)
    pl.semaphore_wait(barrier, len(seqs) + len(tms))


def columns(y, h):
    return pl.ds(pl.multiple_of((2 * y + h) * HD, HD), HD)


def dot_t(a, b):
    return lax.dot_general(a, b, (((1,), (1,)), ((), ())), preferred_element_type=jnp.float32)


def fill_table(codes, tab):
    def slots(n, carry):
        pos = (n // 10) * 2 + n % 2
        code = codes[pos, 0, (n % 10) // 2]
        kept = jnp.maximum(code, 0)
        tile = kept % (NY * NZ)
        pi = (tile % NZ) * NY + tile // NZ
        ri = pos * 4 + kept // (NY * NZ)
        tab[POSE, n] = pi
        tab[RGB, n] = ri
        tab[POSE_KEY, n] = jnp.where(code >= 0, pi, -1 - n)
        tab[RGB_KEY, n] = jnp.where(code >= 0, ri, -1 - n)
        return carry

    lax.fori_loop(0, COUNT, slots, 0)

    def chains(n, carry):
        pose_key, rgb_key = tab[POSE_KEY, n], tab[RGB_KEY, n]
        pose_prev, rgb_prev, rgb_last = COUNT, COUNT, COUNT
        for m in range(COUNT):
            same_rgb = tab[RGB_KEY, m] == rgb_key
            early = n > m
            pose_prev = jnp.where((tab[POSE_KEY, m] == pose_key) & early, m, pose_prev)
            rgb_prev = jnp.where(same_rgb & early, m, rgb_prev)
            rgb_last = jnp.where(same_rgb, m, rgb_last)
        tab[POSE_PREV, n] = pose_prev
        tab[RGB_PREV, n] = rgb_prev
        tab[RGB_LAST, n] = rgb_last
        return carry

    lax.fori_loop(0, COUNT, chains, 0)

    def ends(p, carry):
        pose_end, rgb_end = COUNT, COUNT
        for m in range(COUNT):
            pose_end = jnp.where(tab[POSE_KEY, m] == p, m, pose_end)
            rgb_end = jnp.where(tab[RGB_KEY, m] == p, m, rgb_end)
        tab[POSE_END, p] = pose_end
        tab[RGB_END, p] = rgb_end
        return carry

    lax.fori_loop(0, NY * NZ, ends, 0)


def merge(ref, n, before, high, total, inner):
    old = ref[before, 0:1, :]
    top = jnp.maximum(old, high)
    keep = jnp.exp(old - top)
    add = jnp.exp(high - top)
    ref[n, 0:1, :] = top
    ref[n, 1:2, :] = ref[before, 1:2, :] * keep + total * add
    ref[n, 2:3, :] = ref[before, 2:3, :] * keep + inner * add


def slot_stats(n, tab, factor, qg, pose):
    pi, ri = tab[POSE, n], tab[RGB, n]
    q = qg[ri, 0]
    g = qg[ri, 1]
    both = pose[pi].reshape(2 * TILE, HD)
    pf = pose[pi, 0]
    dots = dot_t(q, both)
    score = dots[:, :TILE] * factor
    high = jnp.max(score, axis=0, keepdims=True)
    w = jnp.exp(score - high)
    pose_new = (
        high,
        jnp.sum(w, axis=0, keepdims=True),
        jnp.sum(w * dots[:, TILE:], axis=0, keepdims=True),
    )
    dots = dot_t(pf, qg[ri].reshape(2 * TILE, HD))
    score = dots[:, :TILE] * factor
    high = jnp.max(score, axis=0, keepdims=True)
    w = jnp.exp(score - high)
    rgb_new = (
        high,
        jnp.sum(w, axis=0, keepdims=True),
        jnp.sum(w * dots[:, TILE:], axis=0, keepdims=True),
    )
    return pose_new, rgb_new


TURNED = (((0,), (0,)), ((), ()))


def slot_before(n, tab, factor, qg, pose, rs):
    pi, ri = tab[POSE, n], tab[RGB, n]
    last = tab[RGB_LAST, n]
    inverse = 1.0 / jnp.maximum(rs[last, 1:2, :], 1.0)
    rows = jnp.concatenate(
        [rs[last, 0:1, :], inverse, rs[last, 2:3, :] * inverse, jnp.zeros((5, HD), jnp.float32)],
        axis=0,
    )
    rows = jnp.transpose(rows)
    q = qg[ri, 0]
    g = qg[ri, 1]
    both = pose[pi].reshape(2 * TILE, HD)
    dots = dot_t(q, both)
    score = dots[:, :TILE] * factor
    grad = dot_t(g, pose[pi, 0])
    pr = jnp.exp(score - rows[:, 0:1]) * rows[:, 1:2]
    own = pr * (grad - rows[:, 2:3])
    part = lax.dot_general(
        pr.astype(jnp.bfloat16), g, TURNED, preferred_element_type=jnp.float32
    )
    return score, own, dots[:, TILE:], part


def slot_after(n, tab, factor, qg, pose, fin, keep):
    pi, ri = tab[POSE, n], tab[RGB, n]
    zz, yy = pi // NY, pi % NY
    score = keep[0, n]
    pp = jnp.exp(score - fin[zz, pl.ds(yy, 1), :]) * fin[zz, pl.ds(4 + yy, 1), :]
    ds = keep[1, n] + pp * (keep[2, n] - fin[zz, pl.ds(8 + yy, 1), :])
    scale_part = jnp.sum((ds * score).reshape(TILE // 8, 8, HD), axis=0)
    scale_part = jnp.where(tab[POSE_KEY, n] >= 0, scale_part, 0.0)
    ds_low = (ds * factor).astype(jnp.bfloat16)
    pair = jnp.concatenate([ds_low, pp.astype(jnp.bfloat16)], axis=1)
    rgb_part = jnp.dot(
        pair, pose[pi].reshape(2 * TILE, HD), preferred_element_type=jnp.float32
    )
    pose_part = lax.dot_general(ds_low, qg[ri, 0], TURNED, preferred_element_type=jnp.float32)
    return rgb_part, pose_part, scale_part


def fused_kernel(
    rgb_ref, cot_ref, pf_ref, pc_ref, pairs_ref, scale,
    rgb_grad, pose_grad, scale_out, pairs_x,
    qg, pose, st, rs, keep, ex, got, fin, racc, pacc, sacc,
    rgbs, rbuf, sbuf, fbuf, land, sc, s_z, s_y, s_t, codes, tab,
    own_sem, codes_sem, y_send, y_recv, z_send, z_recv, b_send, b_recv,
    e1_send, e1_recv, e2_send, e2_recv,
    o_own, o_send, o_recv, r_send, r_recv, l_send, l_recv,
    sz_send, sz_recv, sy_send, sy_recv, st_send, st_recv,
):
    y, z = place()
    t = lax.axis_index("tm")
    sent = []

    def start(copy):
        copy.start()
        sent.append(copy)

    def y_parts(k):
        to = (y + k) % NY
        pos = 3 - k
        parts = [(pairs_ref, pairs_x.at[pos])]
        for h in range(2):
            cols = columns(to, h)
            parts += [
                (pf_ref.at[:, cols], pose[h].at[z * NY + y, 0]),
                (pc_ref.at[:, cols], pose[h].at[z * NY + y, 1]),
                (rgb_ref.at[:, :, cols], qg[h].at[pl.ds(pos * 4, 4), 0]),
                (cot_ref.at[:, :, cols], qg[h].at[pl.ds(pos * 4, 4), 1]),
            ]
        return parts

    def own(i):
        src, dst = y_parts(0)[i]
        return pltpu.make_async_copy(src, dst, own_sem.at[i])

    def across(k, i):
        src, dst = y_parts(k)[i]
        return remote(src, dst, y_send.at[k - 1, i], y_recv.at[k - 1, i], (y + k) % NY, z)

    def hop(h, side, step, c):
        block = (z + NZ - step) % NZ if side == 0 else (z + step) % NZ
        to = (z + 1) % NZ if side == 0 else (z + NZ - 1) % NZ
        ref = pose[h].at[block * NY + (y + NY - c) % NY]
        return remote(
            ref, ref, z_send.at[h, side, step, c], z_recv.at[h, side, step, c], y, to
        )

    def last_used(side, c):
        return (c < 2) == (side == 0)

    def begin(h, side, i):
        src, dst = y_parts(0)[1 + 4 * h + i]
        to = (z + 1) % NZ if side == 0 else (z + NZ - 1) % NZ
        return remote(src, dst, b_send.at[h, side, i], b_recv.at[h, side, i], y, to)

    def ring(h, step, c):
        if step == 0:
            across(c, 1 + 4 * h).wait_recv()
            across(c, 2 + 4 * h).wait_recv()
        for side in range(2):
            if step == 1 and c == 0:
                begin(h, side, 0).wait_recv()
                begin(h, side, 1).wait_recv()
            elif step > 0:
                hop(h, side, step - 1, c).wait_recv()
            if step < 3 or last_used(side, c):
                start(hop(h, side, step, c))

    def ring_all(h, step):
        for c in CHUNKS:
            ring(h, step, c)

    def ring_end(h):
        for c in range(NY):
            for side in range(2):
                if last_used(side, c):
                    hop(h, side, 3, c).wait_recv()

    def rgb_arrived(h):
        own(1 + 4 * h).wait()
        own(2 + 4 * h).wait()
        for i in (3 + 4 * h, 4 + 4 * h):
            for k in (1, 2, 3):
                across(k, i).wait_recv()
            own(i).wait()

    factor = [scale[2 * y + h] / math.sqrt(HD) for h in range(2)]

    def stats(h, low, high):
        def body(m, carry):
            slots = [STATS_UNROLL * m + u for u in range(STATS_UNROLL)]
            news = [slot_stats(n, tab, factor[h], qg[h], pose[h]) for n in slots]
            for n, (pose_new, rgb_new) in zip(slots, news):
                merge(st[h], n, tab[POSE_PREV, n], *pose_new)
                merge(rs[h], n, tab[RGB_PREV, n], *rgb_new)
            return carry

        lax.fori_loop(low, high, body, 0)

    def before(h, low, high):
        def body(m, carry):
            slots = [UNROLL * m + u for u in range(UNROLL)]
            news = [slot_before(n, tab, factor[h], qg[h], pose[h], rs[h]) for n in slots]
            for n, new in zip(slots, news):
                for i in range(3):
                    keep[i, n] = new[i]
                pacc[h][n] = new[3]
            return carry

        lax.fori_loop(low, high, body, 0)

    def after(h, low, high):
        def body(m, carry):
            slots = [UNROLL * m + u for u in range(UNROLL)]
            news = [slot_after(n, tab, factor[h], qg[h], pose[h], fin[h], keep) for n in slots]
            for n, new in zip(slots, news):
                racc[h][n] = racc[h][tab[RGB_PREV, n]] + new[0]
                pacc[h][n] = pacc[h][tab[POSE_PREV, n]] + (pacc[h][n] + new[1])
            sacc[h] += sum(new[2] for new in news)
            return carry

        lax.fori_loop(low, high, body, 0)

    def ex_copy(h, k):
        to = (z + k) % NZ
        return remote(
            ex[h].at[to], got[h].at[z], e1_send.at[h, k - 1], e1_recv.at[h, k - 1], y, to
        )

    def fin_copy(h, k):
        ref = fin[h].at[z]
        return remote(ref, ref, e2_send.at[h, k - 1], e2_recv.at[h, k - 1], y, (z + k) % NZ)

    def ex_first(h):
        def pack(zz):
            for yy in range(NY):
                last = tab[POSE_END, zz * NY + yy]
                for i in range(3):
                    ex[h][zz, 4 * i + yy:4 * i + yy + 1, :] = st[h][last, i:i + 1, :]

        for k in FAR:
            pack((z + k) % NZ)
            start(ex_copy(h, k))
        pack(z)
        got[h][z] = ex[h][z]

    def ex_second(h):
        for k in range(1, NZ):
            ex_copy(h, k).wait_recv()
        top = got[h][0, 0:4, :]
        for k in range(1, NZ):
            top = jnp.maximum(top, got[h][k, 0:4, :])
        total = jnp.zeros_like(top)
        inner = jnp.zeros_like(top)
        for k in range(NZ):
            keep = jnp.exp(got[h][k, 0:4, :] - top)
            total += got[h][k, 4:8, :] * keep
            inner += got[h][k, 8:12, :] * keep
        inverse = 1.0 / jnp.maximum(total, 1.0)
        fin[h][z, 0:4, :] = top
        fin[h][z, 4:8, :] = inverse
        fin[h][z, 8:12, :] = inner * inverse
        for k in FAR:
            start(fin_copy(h, k))

    def ex_end(h):
        for k in range(1, NZ):
            fin_copy(h, k).wait_recv()

    def rgb_copy(h, pos):
        src = rgbs[h].at[pos]
        dst = rgb_grad.at[:, :, columns(y, h)]
        if pos == 3:
            return pltpu.make_async_copy(src, dst, o_own.at[h])
        return remote(src, dst, o_send.at[h, pos], o_recv.at[h, pos], (y + 1 + pos) % NY, z)

    def rgb_send(h, pos):
        for i in range(4):
            rgbs[h][pos, i] = racc[h][tab[RGB_END, pos * 4 + i]].astype(jnp.bfloat16)
        rgb_copy(h, pos).start()

    def goal(side, step):
        return (z + 4 - step) % NZ if side == 0 else (z + 4 + step) % NZ

    def back(h, side, step, c):
        to = (z + 1) % NZ if side == 0 else (z + NZ - 1) % NZ
        if step == 3:
            return remote(
                sbuf[h].at[side, step, c], land[h].at[side, c],
                l_send.at[h, side, c], l_recv.at[h, side, c], (y + c) % NY, to,
            )
        return remote(
            sbuf[h].at[side, step, c], rbuf[h].at[side, step, c],
            r_send.at[h, side, step, c], r_recv.at[h, side, step, c], y, to,
        )

    def straight(h, c):
        return remote(
            fbuf[h].at[c], land[h].at[2, c], l_send.at[h, 2, c], l_recv.at[h, 2, c],
            (y + c) % NY, z,
        )

    def mine(h, block, c):
        return pacc[h][tab[POSE_END, block * NY + (y + c) % NY]]

    def back_one(h, side, step, c):
        value = mine(h, goal(side, step), c)
        if step > 1 or (step == 1 and last_used(side, c)):
            back(h, side, step - 1, c).wait_recv()
            value = value + rbuf[h][side, step - 1, c].astype(jnp.float32)
        sbuf[h][side, step, c] = value.astype(jnp.bfloat16)
        start(back(h, side, step, c))

    def back_step(h, phase):
        for late in range(2):
            step = phase + late
            if step > 3:
                continue
            for i in range(2):
                for side in range(2):
                    c = i + 2 * ((side + late) % 2)
                    back_one(h, side, step, c)
        if phase == 0:
            for c in range(1, NY):
                fbuf[h][c] = mine(h, z, c).astype(jnp.bfloat16)
                start(straight(h, c))

    def back_end(h):
        for c in (2, 3, 1, 0):
            if c == 0:
                value = mine(h, z, c)
            else:
                straight(h, c).wait_recv()
                value = land[h][2, c].astype(jnp.float32)
            for side in range(2):
                back(h, side, 3, c).wait_recv()
                value = value + land[h][side, c].astype(jnp.float32)
            pose_grad[:, columns((y + NY - c) % NY, h)] = value.astype(jnp.bfloat16)

    def z_scale(k):
        return remote(sc, s_z.at[z], sz_send.at[k - 1], sz_recv.at[k - 1], y, (z + k) % NZ)

    def y_scale(k):
        ref = s_y.at[y]
        return remote(ref, ref, sy_send.at[k - 1], sy_recv.at[k - 1], (y + k) % NY, z)

    def t_scale(k):
        ref = s_t.at[t]
        return remote_tm(ref, ref, st_send.at[k - 1], st_recv.at[k - 1], (t + k) % NT)

    def total_of(ref, count):
        total = ref[0]
        for k in range(1, count):
            total = total + ref[k]
        return total

    def scale_first():
        lane = lax.broadcasted_iota(jnp.int32, (8, HD), 1)
        tile = jnp.zeros((8, HD), jnp.float32)
        for h in range(2):
            part = jnp.sum(sacc[h], axis=0, keepdims=True)
            part = jnp.sum(part, axis=1, keepdims=True) / scale[2 * y + h]
            tile = jnp.where(lane == 2 * y + h, part, tile)
        sc[...] = tile
        for k in FAR:
            start(z_scale(k))
        s_z[z] = tile

    def scale_second():
        for k in range(1, NZ):
            z_scale(k).wait_recv()
        s_y[y] = total_of(s_z, NZ)
        for k in ACROSS:
            start(y_scale(k))

    def scale_third():
        for k in range(1, NY):
            y_scale(k).wait_recv()
        s_t[t] = total_of(s_y, NY)
        for k in FAR:
            start(t_scale(k))

    def scale_end():
        for k in range(1, NT):
            t_scale(k).wait_recv()
        scale_out[...] = total_of(s_t, NT)

    greet(
        [(y, (z + k) % NZ) for k in FAR]
        + [((y + k) % NY, (z + side) % NZ) for k in ACROSS for side in (1, NZ - 1)]
        + [((y + k) % NY, z) for k in ACROSS],
        [(t + k) % NT for k in FAR],
    )
    for h in range(2):
        for i in range(2):
            for side in range(2):
                start(begin(h, side, i))
        for i in (1 + 4 * h, 2 + 4 * h):
            for k in ACROSS:
                start(across(k, i))
    for k in (1, 2, 3):
        start(across(k, 0))
    for i in (0, 1, 2, 5, 6):
        own(i).start()
    for h in range(2):
        st[h][COUNT, 0:1, :] = jnp.full((1, HD), NEG, jnp.float32)
        rs[h][COUNT, 0:1, :] = jnp.full((1, HD), NEG, jnp.float32)
        st[h][COUNT, 1:3, :] = jnp.zeros((2, HD), jnp.float32)
        rs[h][COUNT, 1:3, :] = jnp.zeros((2, HD), jnp.float32)
        racc[h][COUNT] = jnp.zeros((TILE, HD), jnp.float32)
        pacc[h][COUNT] = jnp.zeros((TILE, HD), jnp.float32)
        sacc[h] = jnp.zeros((8, HD), jnp.float32)
    for c in CHUNKS[1:]:
        ring(0, 0, c)
    for i in (3, 4):
        for k in ACROSS:
            start(across(k, i))
        own(i).start()
    for k in (1, 2, 3):
        across(k, 0).wait_recv()
    own(0).wait()
    to_codes = pltpu.make_async_copy(pairs_x, codes, codes_sem.at[0])
    to_codes.start()
    to_codes.wait()
    ring_all(0, 1)
    fill_table(codes, tab)
    ring_all(0, 2)
    ring_all(0, 3)
    for c in CHUNKS[1:]:
        ring(1, 0, c)
    for i in (7, 8):
        for k in ACROSS:
            start(across(k, i))
        own(i).start()
    ring_end(0)
    rgb_arrived(0)
    ring(1, 1, CHUNKS[0])
    stats(0, 0, 1)
    ring(1, 1, CHUNKS[1])
    stats(0, 1, 2)
    ring(1, 1, CHUNKS[2])
    ex_first(0)
    ring(1, 1, CHUNKS[3])
    before(0, 0, 1)
    ring(1, 2, CHUNKS[0])
    before(0, 1, 2)
    ring(1, 2, CHUNKS[1])
    before(0, 2, 3)
    ring(1, 2, CHUNKS[2])
    ex_second(0)
    ring(1, 2, CHUNKS[3])
    before(0, 3, 4)
    for c in CHUNKS:
        ring(1, 3, c)
    ex_end(0)
    after(0, 0, 4)
    back_step(0, 0)
    for pos in range(4):
        rgb_send(0, pos)
    ring_end(1)
    rgb_arrived(1)
    stats(1, 0, 2)
    ex_first(1)
    back_step(0, 1)
    before(1, 0, 2)
    back_step(0, 2)
    ex_second(1)
    before(1, 2, 4)
    back_step(0, 3)
    ex_end(1)
    after(1, 0, 4)
    back_step(1, 0)
    scale_first()
    for pos in range(4):
        rgb_send(1, pos)
    back_step(1, 1)
    scale_second()
    back_end(0)
    back_step(1, 2)
    scale_third()
    back_step(1, 3)
    back_end(1)
    scale_end()
    for h in range(2):
        for pos in range(4):
            rgb_copy(h, pos).wait()
    for copy in sent:
        copy.wait_send()


def fused(rgb, cot, pf, pc, pairs, scale):
    dma = pltpu.SemaphoreType.DMA
    low, full = jnp.bfloat16, jnp.float32

    def twice(shape, kind):
        return [pltpu.VMEM(shape, kind)] * 2

    return pl.pallas_call(
        fused_kernel,
        out_shape=(
            jax.ShapeDtypeStruct((4, TILE, 1024), low),
            jax.ShapeDtypeStruct((TILE, 1024), low),
            jax.ShapeDtypeStruct((8, HD), full),
            jax.ShapeDtypeStruct((NY, 1, SLOTS), jnp.int32),
        ),
        in_specs=[HBM] * 5 + [SM],
        out_specs=(VM, VM, VM, HBM),
        scratch_shapes=[
            twice((16, 2, TILE, HD), low),
            twice((NY * NZ, 2, TILE, HD), low),
            twice((COUNT + 1, 8, HD), full),
            twice((COUNT + 1, 8, HD), full),
            pltpu.VMEM((3, COUNT, TILE, HD), full),
            twice((NZ, 16, HD), full),
            twice((NZ, 16, HD), full),
            twice((NZ, 16, HD), full),
            twice((COUNT + 1, TILE, HD), full),
            twice((COUNT + 1, TILE, HD), full),
            pltpu.VMEM((2, 8, HD), full),
            twice((4, 4, TILE, HD), low),
            twice((2, 3, NY, TILE, HD), low),
            twice((2, 4, NY, TILE, HD), low),
            twice((NY, TILE, HD), low),
            twice((3, NY, TILE, HD), low),
            pltpu.VMEM((8, HD), full),
            pltpu.VMEM((NZ, 8, HD), full),
            pltpu.VMEM((NY, 8, HD), full),
            pltpu.VMEM((NT, 8, HD), full),
            pltpu.SMEM((NY, 1, SLOTS), jnp.int32),
            pltpu.SMEM((9, NY * NZ), jnp.int32),
            dma((9,)), dma((1,)), dma((3, 9)), dma((3, 9)),
            dma((2, 2, 4, NY)), dma((2, 2, 4, NY)), dma((2, 2, 2)), dma((2, 2, 2)),
            dma((2, NZ - 1)), dma((2, NZ - 1)), dma((2, NZ - 1)), dma((2, NZ - 1)),
            dma((2,)), dma((2, 3)), dma((2, 3)),
            dma((2, 2, 3, NY)), dma((2, 2, 3, NY)),
            dma((2, 3, NY)), dma((2, 3, NY)),
            dma((NZ - 1,)), dma((NZ - 1,)),
            dma((NY - 1,)), dma((NY - 1,)),
            dma((NT - 1,)), dma((NT - 1,)),
        ],
        compiler_params=pltpu.CompilerParams(
            collective_id=0, has_side_effects=True, vmem_limit_bytes=VMEM_LIMIT
        ),
    )(rgb, cot, pf, pc, pairs, scale)


def finish_kernel(rgb, pose, scale, rgb_out, pose_out, scale_out, sem):
    copies = [
        pltpu.make_async_copy(rgb.at[i], rgb_out.at[i], sem.at[i]) for i in range(4)
    ] + [pltpu.make_async_copy(pose, pose_out, sem.at[4])]
    for copy in copies:
        copy.start()
    scale_out[...] = scale[0:1, 0:8]
    for copy in copies:
        copy.wait()


def finish(rgb, pose, scale):
    return pl.pallas_call(
        finish_kernel,
        out_shape=(
            jax.ShapeDtypeStruct(rgb.shape, rgb.dtype),
            jax.ShapeDtypeStruct(pose.shape, pose.dtype),
            jax.ShapeDtypeStruct((1, 8), jnp.float32),
        ),
        in_specs=[VM, VM, VM],
        out_specs=(HBM, HBM, VM),
        scratch_shapes=[pltpu.SemaphoreType.DMA((5,))],
        compiler_params=pltpu.CompilerParams(vmem_limit_bytes=VMEM_LIMIT),
    )(rgb, pose, scale)


def local(rgb_feat, rgb_grad_out, pose_feat, pose_grad_out, logit_scale, pairs):
    rgb_grad, pose_grad, scale_grad, _ = fused(
        *(
            pltpu.with_memory_space_constraint(part, pltpu.HBM)
            for part in (
                rgb_feat.reshape(4, TILE, 1024),
                rgb_grad_out.reshape(4, TILE, 1024),
                pose_feat[0],
                pose_grad_out[0],
                pairs,
            )
        ),
        pltpu.with_memory_space_constraint(logit_scale, pltpu.HBM),
    )
    rgb_grad, pose_grad, scale_grad = finish(rgb_grad, pose_grad, scale_grad)
    return rgb_grad.reshape(1, 512, 1024), pose_grad[None], scale_grad[0]


def solution(mesh):
    return jax.shard_map(
        local,
        mesh=mesh,
        in_specs=(
            P("tm", "seq", None),
            P("tm", "seq", None),
            P("tm", "seq", None),
            P("tm", "seq", None),
            P(),
            P("tm", "seq"),
        ),
        out_specs=(P("tm", "seq", None), P("tm", "seq", None), P()),
        check_vma=False,
    )
```
